128 devices in a mesh: ulysses: 4 (over z_hi, core), blk: 32 (over y, z_lo, x).
Axes of the slice: x: 4, y: 4, z: 4 (z_hi: 2, z_lo: 2; z = z_hi * 2 + z_lo), core: 2. Of those that a mesh axis runs over, the one named last changes fastest.
Arguments:
- query_in: bfloat16 [13312, 2560], P(('ulysses', 'blk')), may hold values from -160 to 160
- key_in: bfloat16 [13312, 2560], P(('ulysses', 'blk')), may hold values from -10 to 10
- value_in: bfloat16 [13312, 2560], P(('ulysses', 'blk')), may hold values from -12 to 12
- residual: bfloat16 [13312, 5120], P(('ulysses', 'blk')), may hold values from -3 to 3
- out_weight: bfloat16 [2560, 5120], P('ulysses'), may hold values from -0.125 to 0.125
- gate_scale: float32 [5120], replicated, may hold values from 0.5 to 1.5
Outputs:
- mixed: bfloat16 [13312, 5120], P(('ulysses', 'blk'))
The draws below stay inside these ranges and needn't reach their ends.
All inputs are finite; a program needn't handle non-finite values.
Results may differ from the reference program's by a relative error of at most 0.014.
Values may be sent and summed in bfloat16 or wider, within the bound.
No kernel may reach another device: no remote copies, remote signals or barrier semaphores. Data moves between devices by JAX's collectives and lax.ppermute only.
A program may use at most 128 MiB of HBM per device.

```python
import math
import jax
import jax.numpy as jnp
from jax import lax

D = 5120
HEADS = 20
HEAD_DIM = 128
INNER = 2560
TOKENS = 13312


def shared_keys(key):
    return 1.6 * jax.random.truncated_normal(key, -6.0, 6.0, (TOKENS, INNER), jnp.float32)


def draw_key_in(key, part):
    shared = shared_keys(key)
    return shared.astype(jnp.bfloat16)


def draw_query_in(key, part):
    key = jax.random.fold_in(key, 7)
    own_key = jax.random.fold_in(key, 0)
    result = 1.6 * jax.random.truncated_normal(own_key, -6.0, 6.0, (TOKENS, INNER), jnp.float32)
    return result.astype(jnp.bfloat16)


def block_levels(stream_key, dims, cuts, low, top_value):
    def one(axis_at, blocks):
        draws = jax.random.uniform(jax.random.fold_in(jax.random.fold_in(stream_key, 6), axis_at), (blocks,), jnp.float32, low / len(cuts), top_value / len(cuts))
        return jnp.repeat(jnp.exp(draws), dims[axis_at] // blocks).reshape((-1,) + (1,) * (len(dims) - axis_at - 1))

    gain = one(*cuts[0])
    for cut in cuts[1:]:
        gain = gain * one(*cut)
    return gain


def normal_values(stream_key, shape, spread, most, cuts=(), held_as=jnp.bfloat16):
    loudness = block_levels(stream_key, shape, cuts, -0.22, 0.18) if cuts else 1.0
    drawn = jax.random.normal(stream_key, shape, jnp.float32) * spread * loudness
    return jnp.minimum(jnp.maximum(drawn, -most), most).astype(held_as)


def setup_inputs(seed: int = 0) -> dict:
    key_list = jax.random.split(jax.random.key(seed), 7)
    query_in = draw_query_in(jax.random.fold_in(key_list[6], 71), 0)
    key_in = draw_key_in(jax.random.fold_in(key_list[6], 71), 0)
    value_in = normal_values(key_list[2], (TOKENS, INNER), 2.0, 12.0, ((0, 128),))
    residual = normal_values(key_list[3], (TOKENS, D), 0.5, 3.0, ((0, 128),))
    out_weight = normal_values(key_list[4], (INNER, D), INNER ** -0.5, 0.125, ((0, 4),))
    gate_scale = jnp.clip(jax.random.uniform(key_list[5], (D,), jnp.float32, 0.5, 1.5), 0.5, 1.5)
    return {"query_in": query_in, "key_in": key_in, "value_in": value_in, "residual": residual, "out_weight": out_weight, "gate_scale": gate_scale}


def attend_block(query_block, keys_head, values_head):
    scores = jnp.dot(query_block, keys_head.T, preferred_element_type=jnp.float32) * (HEAD_DIM ** -0.5)
    largest = jnp.max(scores, axis=-1, keepdims=True)
    weights = jnp.exp(scores - largest)
    totals = jnp.sum(weights, axis=-1, keepdims=True)
    summed = jnp.dot(weights.astype(jnp.bfloat16), values_head, preferred_element_type=jnp.float32)
    return summed / totals


def by_heads(source):
    return source.reshape(TOKENS, HEADS, HEAD_DIM).transpose(1, 0, 2)


def reference(query_in, key_in, value_in, residual, out_weight, gate_scale):
    block_rows = math.gcd(TOKENS, 1024)

    def per_head(operands):
        query_head, keys_head, values_head = operands
        blocks = query_head.reshape(TOKENS // block_rows, block_rows, HEAD_DIM)
        outcome = lax.map(lambda query_block: attend_block(query_block, keys_head, values_head), blocks)
        return outcome.reshape(TOKENS, HEAD_DIM)

    outcome = lax.map(per_head, (by_heads(query_in), by_heads(key_in), by_heads(value_in)))
    attended = outcome.transpose(1, 0, 2).reshape(TOKENS, INNER).astype(jnp.bfloat16)
    projected = jnp.dot(attended, out_weight, preferred_element_type=jnp.float32)
    return (residual.astype(jnp.float32) + gate_scale * projected).astype(jnp.bfloat16)
```

```python
import functools

import jax
import jax.numpy as jnp
from jax import lax
from jax.experimental import pallas as pl
from jax.experimental.pallas import tpu as pltpu
from jax.sharding import Mesh
from jax.sharding import PartitionSpec as P

HEAD_DIM = 128
LANES = 128
SCALE = HEAD_DIM**-0.5 * 1.4426950408889634
ALL = ("zh", "c", "y", "zl", "x")
Z = ("zh", "zl")
KEY_TILE = 256
SETS = (((0, 3), "y", "x"), ((3, 5), "x", "y"))


def shift(x, axis, by):
    devices = lax.axis_size(axis)
    return lax.ppermute(x, axis, [(i, (i + by) % devices) for i in range(devices)])


def swap_core(x):
    return lax.ppermute(x, "c", [(0, 1), (1, 0)])


def flash_body(heads, rows, *refs):
    q_refs, key_refs, value_refs = refs[:4], refs[4:12], refs[12:20]
    out_refs = refs[20:24]
    keys, values = refs[24:]
    head = pl.program_id(0)

    @pl.when(head == 0)
    def _():
        values[:, HEAD_DIM:] = jnp.ones((8 * rows, LANES), jnp.bfloat16)
        for out in out_refs:
            out[:, heads * LANES :] = jnp.zeros((rows, LANES), jnp.bfloat16)

    for i in range(8):
        part = pl.ds(i * rows, rows)
        keys[part, :] = key_refs[i][...].reshape(rows, HEAD_DIM)
        values[part, :HEAD_DIM] = value_refs[i][...].reshape(rows, HEAD_DIM)
    lane = lax.broadcasted_iota(jnp.int32, (rows, LANES), 1)
    for q_ref, out in zip(q_refs, out_refs):
        q = q_ref[...]
        largest = None
        for j in range(8 * rows // KEY_TILE):
            part = pl.ds(j * KEY_TILE, KEY_TILE)
            scores = lax.dot_general(
                q, keys[part, :], (((1,), (1,)), ((), ())), preferred_element_type=jnp.float32
            )
            here = jnp.max(scores, axis=1, keepdims=True)
            new = here if largest is None else jnp.maximum(largest, here)
            weights = jnp.exp2((scores - new) * SCALE).astype(jnp.bfloat16)
            update = jnp.dot(weights, values[part, :], preferred_element_type=jnp.float32)
            if largest is None:
                total = update
            else:
                total = total * jnp.exp2((largest - new) * SCALE) + update
            largest = new
        out[:, pl.ds(pl.multiple_of(head * LANES, LANES), LANES)] = (
            total[:, :HEAD_DIM] / total[:, HEAD_DIM:]
        ).astype(jnp.bfloat16)
        level = largest * SCALE + jnp.log2(total[:, HEAD_DIM:])
        high = level.astype(jnp.bfloat16)
        rest = level - high.astype(jnp.float32)
        middle = rest.astype(jnp.bfloat16)
        low = (rest - middle.astype(jnp.float32)).astype(jnp.bfloat16)
        block = out[:, heads * LANES :]
        for k, value in enumerate((high, middle, low)):
            block = jnp.where(lane == 3 * head + k, value, block)
        out[:, heads * LANES :] = block


def flash(queries, keys, values, heads, rows):
    def spec(x, which):
        if x.ndim == 2:
            return pl.BlockSpec((rows, HEAD_DIM), lambda h: (0, h))
        return pl.BlockSpec((1, rows, HEAD_DIM), lambda h: (which, 0, h))

    pairs = 4 * rows * 8 * rows * heads
    out = jax.ShapeDtypeStruct((rows, (heads + 1) * LANES), jnp.bfloat16)
    return pl.pallas_call(
        functools.partial(flash_body, heads, rows),
        grid=(heads,),
        out_shape=[out] * 4,
        in_specs=[spec(x, 0) for x in queries]
        + [spec(x, 0) for x in keys]
        + [spec(x, 1) for x in values],
        out_specs=[pl.BlockSpec(out.shape, lambda h: (0, 0))] * 4,
        scratch_shapes=[
            pltpu.VMEM((8 * rows, HEAD_DIM), jnp.bfloat16),
            pltpu.VMEM((8 * rows, 2 * HEAD_DIM), jnp.bfloat16),
        ],
        compiler_params=pltpu.CompilerParams(vmem_limit_bytes=48 << 20),
        cost_estimate=pl.CostEstimate(
            flops=8 * pairs * HEAD_DIM, bytes_accessed=24 * rows * heads * 256, transcendentals=pairs
        ),
    )(*queries, *keys, *values)


def merge_body(heads_per_set, *refs):
    out = refs[-1]
    at = 0
    for s, heads in enumerate(heads_per_set):
        parts = refs[4 * s : 4 * s + 4]
        blocks = [p[:, heads * LANES :].astype(jnp.float32) for p in parts]
        for h in range(heads):
            levels = [
                b[:, 3 * h : 3 * h + 1] + b[:, 3 * h + 1 : 3 * h + 2] + b[:, 3 * h + 2 : 3 * h + 3]
                for b in blocks
            ]
            top = functools.reduce(jnp.maximum, levels)
            shares = [jnp.exp2(v - top) for v in levels]
            whole = shares[0] + shares[1] + shares[2] + shares[3]
            lanes = slice(h * LANES, (h + 1) * LANES)
            total = sum(w * p[:, lanes].astype(jnp.float32) for w, p in zip(shares, parts))
            out[:, at * LANES : (at + 1) * LANES] = (total / whole).astype(jnp.bfloat16)
            at += 1


def merge(parts, heads_per_set, rows):
    return pl.pallas_call(
        functools.partial(merge_body, heads_per_set),
        out_shape=jax.ShapeDtypeStruct((rows, sum(heads_per_set) * LANES), jnp.bfloat16),
        compiler_params=pltpu.CompilerParams(vmem_limit_bytes=48 << 20),
    )(*parts)


def on_device(query_in, key_in, value_in, residual, out_weight, gate_scale):
    own_rows = query_in.shape[0]
    rows = 4 * own_rows
    group = query_in.shape[1] // 4
    other_weight = swap_core(out_weight)
    zh, zl, core = lax.axis_index("zh"), lax.axis_index("zl"), lax.axis_index("c")

    parts, heads_per_set = [], []
    for (first, last), key_axis, query_axis in SETS:
        heads = last - first
        lanes = slice(first * LANES, last * LANES)
        cut = lambda x: x.reshape(own_rows, 4, group)[:, :, lanes].transpose(1, 0, 2)
        sent = jnp.stack([cut(query_in), cut(key_in), cut(value_in)], axis=1)
        got = lax.all_to_all(sent, Z, split_axis=0, concat_axis=0, tiled=True)
        q = got[:, 0].reshape(rows, heads * LANES)
        kv = got[:, 1:].transpose(1, 0, 2, 3).reshape(2, rows, heads * LANES)
        left, right = shift(kv, key_axis, 1), shift(kv, key_axis, -1)
        far_k, far_v = shift(left[0], key_axis, 1), shift(right[1], key_axis, -1)
        mine = (kv, left, right)
        other = tuple(swap_core(x) for x in mine)
        keys = mine + (far_k,) + other + (swap_core(far_k),)
        values = mine + (far_v,) + other + (swap_core(far_v),)
        queries = (q, shift(q, query_axis, 1), shift(q, query_axis, -1), shift(q, query_axis, 2))
        o = flash(queries, keys, values, heads, rows)
        parts += [
            o[0],
            shift(o[1], query_axis, -1),
            shift(o[2], query_axis, 1),
            shift(o[3], query_axis, 2),
        ]
        heads_per_set.append(heads)
    attended = merge(parts, tuple(heads_per_set), rows).reshape(4, own_rows, group)

    outer = zh == zl
    ends = jnp.stack([attended[0], attended[3]])
    middle = jnp.stack([attended[1], attended[2]])
    kept = jnp.where(outer, ends, middle).reshape(2 * own_rows, group)
    given = jnp.where(outer, middle, ends).reshape(2 * own_rows, group)
    taken = lax.ppermute(given, "zl", [(0, 1), (1, 0)])
    same = zl == core
    for_own = jnp.where(same, kept, taken)
    for_other = jnp.where(same, taken, kept)
    partial = jnp.dot(for_own, out_weight, preferred_element_type=jnp.float32) + jnp.dot(
        for_other, other_weight, preferred_element_type=jnp.float32
    )
    low, high = partial[:own_rows], partial[own_rows:]
    theirs = jnp.where(zh == 0, high, low).astype(jnp.bfloat16)
    mine = jnp.where(zh == 0, low, high)
    arrived = lax.ppermute(theirs, Z, [(i, 3 - i) for i in range(4)])
    projected = mine + arrived.astype(jnp.float32)
    return (residual.astype(jnp.float32) + gate_scale * projected).astype(jnp.bfloat16)


def solution(mesh):
    fine = Mesh(mesh.devices.reshape(2, 2, 4, 2, 4), ALL)
    tokens = P(ALL, None)
    return jax.shard_map(
        on_device,
        mesh=fine,
        in_specs=(tokens, tokens, tokens, tokens, P(("zh", "c"), None), P()),
        out_specs=tokens,
        check_vma=False,
    )
```

```python
import functools

import jax
import jax.numpy as jnp
from jax import lax
from jax.experimental import pallas as pl
from jax.experimental.pallas import tpu as pltpu
from jax.sharding import Mesh
from jax.sharding import PartitionSpec as P

HEAD_DIM = 128
LANES = 128
SCALE = HEAD_DIM**-0.5 * 1.4426950408889634
ALL = ("zh", "c", "y", "zl", "x")
SIZES = {"zh": 2, "c": 2, "y": 4, "zl": 2, "x": 4}
Z = ("zh", "zl")
CZ = ("c", "zh", "zl")
KEY_TILE = 256
LEVEL_ROWS = 16
F32 = jnp.float32
BF16 = jnp.bfloat16
NT = (((1,), (1,)), ((), ()))


def move(x, place):
    pairs = []
    for at in range(128):
        left, coords = at, {}
        for name in reversed(ALL):
            left, coords[name] = divmod(left, SIZES[name])
        target = place(dict(coords))
        to = 0
        for name in ALL:
            to = to * SIZES[name] + target[name] % SIZES[name]
        pairs.append((at, to))
    return lax.ppermute(x, ALL, pairs)


def along(x, by, keys):
    def place(at):
        at["y" if (at["c"] == 0) == keys else "x"] += by
        return at

    return move(x, place)


def flip(x, *names):
    return move(x, lambda at: {n: 1 - v if n in names else v for n, v in at.items()})


def cut_body(q, k, v, shared, first, second):
    for i, x in enumerate((q, k, v)):
        for z in range(4):
            for out, heads in ((shared, (4,)), (first, (0, 2)), (second, (1, 3))):
                for c, head in enumerate(heads):
                    lanes = slice((5 * z + head) * LANES, (5 * z + head + 1) * LANES)
                    out[4 * c + z, i] = x[:, lanes]


def cut(q, k, v):
    rows = q.shape[0]
    return pl.pallas_call(
        cut_body,
        out_shape=[jax.ShapeDtypeStruct((n, 3, rows, LANES), BF16) for n in (4, 8, 8)],
    )(q, k, v)


def eye(rows):
    return lax.broadcasted_iota(jnp.int32, (rows, LANES), 0) == lax.broadcasted_iota(
        jnp.int32, (rows, LANES), 1
    )


def write_levels(out, at, level):
    rows = level.shape[0]
    lines = []
    for start in range(0, rows, LANES):
        piece = level[start : start + LANES]
        lines.append(jnp.sum(jnp.where(eye(piece.shape[0]), piece, 0.0), axis=0, keepdims=True))
    line = jnp.concatenate(lines, axis=0)
    high = line.astype(BF16).astype(F32)
    middle = (line - high).astype(BF16).astype(F32)
    low = line - high - middle
    spare = jnp.zeros((LEVEL_ROWS - 3 * len(lines), LANES), F32)
    out[at, rows:, :] = jnp.concatenate([high, middle, low, spare], axis=0).astype(BF16)


def read_levels(block, rows):
    n = -(-rows // LANES)
    parts = block[rows:, :].astype(F32)
    return parts[:n] + parts[n : 2 * n] + parts[2 * n : 3 * n]


def column(line, rows):
    pieces = []
    for i, start in enumerate(range(0, rows, LANES)):
        here = min(LANES, rows - start)
        wide = jnp.broadcast_to(line[i : i + 1], (here, LANES))
        pieces.append(jnp.sum(jnp.where(eye(here), wide, 0.0), axis=1, keepdims=True))
    return jnp.concatenate(pieces, axis=0)


def flash_body(n_units, rows, key_rows, *refs):
    q_refs, kv_refs = refs[:n_units], refs[n_units : n_units + 4]
    out, queries, keys, values = refs[n_units + 4 :]
    values[:, HEAD_DIM:] = jnp.ones((4 * key_rows, LANES), BF16)
    for i in range(4):
        part = pl.ds(i * key_rows, key_rows)
        keys[part, :] = kv_refs[i][0]
        values[part, :HEAD_DIM] = kv_refs[i][1]
    for i in range(n_units):
        queries[pl.ds(2 * i * rows, 2 * rows), :] = q_refs[i][...]

    def block(i, _):
        q = queries[pl.ds(pl.multiple_of(i * rows, rows), rows), :]
        largest = total = None
        for start in range(0, 4 * key_rows, KEY_TILE):
            part = pl.ds(start, min(KEY_TILE, 4 * key_rows - start))
            scores = lax.dot_general(q, keys[part, :], NT, preferred_element_type=F32)
            new = jnp.max(scores, axis=1, keepdims=True)
            if total is not None:
                new = jnp.maximum(largest, new)
            weights = jnp.exp2((scores - new) * SCALE).astype(BF16)
            update = jnp.dot(weights, values[part, :], preferred_element_type=F32)
            if total is None:
                total = update
            else:
                total = total * jnp.exp2((largest - new) * SCALE) + update
            largest = new
        sums = total[:, HEAD_DIM:]
        out[i, :rows, :] = (total[:, :HEAD_DIM] / sums).astype(BF16)
        write_levels(out, i, largest * SCALE + jnp.log2(sums))
        return 0

    lax.fori_loop(0, 2 * n_units, block, 0)


def flash(queries, kvs):
    n, rows, key_rows = len(queries), queries[0].shape[0] // 2, kvs[0].shape[1]
    pairs = 2 * n * rows * 4 * key_rows
    out = pl.pallas_call(
        functools.partial(flash_body, n, rows, key_rows),
        out_shape=jax.ShapeDtypeStruct((2 * n, rows + LEVEL_ROWS, LANES), BF16),
        scratch_shapes=[
            pltpu.VMEM((2 * n * rows, HEAD_DIM), BF16),
            pltpu.VMEM((4 * key_rows, HEAD_DIM), BF16),
            pltpu.VMEM((4 * key_rows, 2 * HEAD_DIM), BF16),
        ],
        compiler_params=pltpu.CompilerParams(vmem_limit_bytes=40 << 20),
        cost_estimate=pl.CostEstimate(
            flops=8 * pairs * HEAD_DIM, bytes_accessed=8 * rows * 256 * n, transcendentals=pairs
        ),
    )(*queries, *kvs)
    return [out[2 * i : 2 * i + 2] for i in range(n)]


def merge_blocks(blocks, rows):
    levels = [read_levels(b, rows) for b in blocks]
    top = functools.reduce(jnp.maximum, levels)
    shares = [jnp.exp2(v - top) for v in levels]
    whole = functools.reduce(jnp.add, shares)
    total = 0.0
    for share, b in zip(shares, blocks):
        total = total + column(share / whole, rows) * b[:rows, :].astype(F32)
    return total.astype(BF16), column(top + jnp.log2(whole), rows)


def merge_shared_body(rows, a, b, c, d, mine, other):
    for i, out in enumerate((mine, other)):
        value, level = merge_blocks([x[i] for x in (a, b, c, d)], rows)
        out[0, :rows, :] = value
        write_levels(out, 0, jnp.broadcast_to(level, (rows, LANES)))


def merge_body(rows, a, b, c, d, *rest):
    out = rest[-1] if len(rest) == 1 else rest[2]
    for i in range(2):
        out[i * rows : (i + 1) * rows, :] = merge_blocks([x[i] for x in (a, b, c, d)], rows)[0]
    if len(rest) > 1:
        rest[3][...] = merge_blocks([rest[0][0], rest[1][0]], rows)[0]


def on_device(query_in, key_in, value_in, residual, out_weight, gate_scale):
    own_rows = query_in.shape[0]
    rows = 4 * own_rows
    other_weight = flip(out_weight, "c")
    zh, zl, core = lax.axis_index("zh"), lax.axis_index("zl"), lax.axis_index("c")

    shared, first, second = cut(query_in, key_in, value_in)

    def spread(x, axes):
        got = lax.all_to_all(x, axes, split_axis=0, concat_axis=0, tiled=True)
        return got.transpose(1, 0, 2, 3).reshape(3, got.shape[0] * own_rows, LANES)

    def gather(q, kv):
        return (
            [q, along(q, 1, False), along(q, -1, False), along(q, 2, False)],
            [kv, along(kv, 1, True), along(kv, -1, True), along(kv, 2, True)],
        )

    def send_back(parts):
        return [
            parts[0],
            along(parts[1], -1, False),
            along(parts[2], 1, False),
            along(parts[3], 2, False),
        ]

    got = spread(shared, Z)
    first, got = lax.optimization_barrier((first, got))
    q = jnp.concatenate([got[0], flip(got[0], "c")], axis=0)
    parts = send_back(flash(*gather(q, got[1:])))
    block = jax.ShapeDtypeStruct((1, rows + LEVEL_ROWS, LANES), BF16)
    mine, other = pl.pallas_call(
        functools.partial(merge_shared_body, rows), out_shape=[block, block]
    )(*parts)
    other = flip(other, "c")

    got = spread(first, CZ)
    second, got = lax.optimization_barrier((second, got))
    parts = send_back(flash(*gather(got[0], got[1:])))
    whole = jax.ShapeDtypeStruct((2 * rows, LANES), BF16)
    half = jax.ShapeDtypeStruct((rows, LANES), BF16)
    out_first, out_shared = pl.pallas_call(
        functools.partial(merge_body, rows), out_shape=[whole, half]
    )(*parts, mine, other)

    got = spread(second, CZ)
    queries, kvs = gather(got[0], got[1:])
    away = flash(queries[1:], kvs)
    here = flash(queries[:1], kvs)
    parts = send_back(here + away)
    out_second = pl.pallas_call(functools.partial(merge_body, rows), out_shape=whole)(*parts)

    outer = zh == zl
    pair = jnp.concatenate([out_first, out_second], axis=1).reshape(2, 4, own_rows, 2 * LANES)
    tokens_here = jnp.where(core == 0, pair[0], pair[1])
    tokens_there = jnp.where(core == 0, pair[1], pair[0])
    out_shared = out_shared.reshape(4, own_rows, LANES)

    def pick(x, ends):
        a, b = jnp.where(ends, x[0], x[1]), jnp.where(ends, x[3], x[2])
        return jnp.concatenate([a, b], axis=0)

    tokens_here = jnp.concatenate([tokens_here, out_shared], axis=2)
    kept = pick(tokens_here, outer)
    from_z = flip(pick(tokens_here, ~outer), "zl")
    from_c = flip(pick(tokens_there, outer), "c")
    from_zc = flip(pick(tokens_there, ~outer), "zl", "c")

    def features(own, other):
        w = 2 * LANES
        lo = jnp.where(core == 0, own[:, :w], other)
        hi = jnp.where(core == 0, other, own[:, :w])
        return jnp.concatenate([lo, hi, own[:, w:]], axis=1)

    my_group, next_group = features(kept, from_c), features(from_z, from_zc)
    same = zl == core
    for_own = jnp.where(same, my_group, next_group)
    for_other = jnp.where(same, next_group, my_group)
    partial = jnp.dot(for_own, out_weight, preferred_element_type=F32) + jnp.dot(
        for_other, other_weight, preferred_element_type=F32
    )
    low, high = partial[:own_rows], partial[own_rows:]
    theirs = jnp.where(zh == 0, high, low).astype(BF16)
    ours = jnp.where(zh == 0, low, high)
    projected = ours + flip(theirs, "zh", "zl").astype(F32)
    return (residual.astype(F32) + gate_scale * projected).astype(BF16)


def solution(mesh):
    fine = Mesh(mesh.devices.reshape(tuple(SIZES.values())), ALL)
    tokens = P(ALL, None)
    return jax.shard_map(
        on_device,
        mesh=fine,
        in_specs=(tokens, tokens, tokens, tokens, P(("zh", "c"), None), P()),
        out_specs=tokens,
        check_vma=False,
    )
```

```python
import functools

import jax
import jax.numpy as jnp
from jax import lax
from jax.experimental import pallas as pl
from jax.experimental.pallas import tpu as pltpu
from jax.sharding import Mesh
from jax.sharding import PartitionSpec as P

HEAD_DIM = 128
LANES = 128
SCALE = HEAD_DIM**-0.5 * 1.4426950408889634
ALL = ("zh", "c", "y", "zl", "x")
SIZES = {"zh": 2, "c": 2, "y": 4, "zl": 2, "x": 4}
Z = ("zh", "zl")
CZ = ("c", "zh", "zl")
KEY_TILE = 256
LEVEL_ROWS = 16
F32 = jnp.float32
BF16 = jnp.bfloat16
NT = (((1,), (1,)), ((), ()))


def flip(x, *names):
    total = 2 ** len(names)
    return lax.ppermute(x, names, [(i, total - 1 - i) for i in range(total)])


def exchange(x, axes):
    return lax.all_to_all(x, axes, split_axis=0, concat_axis=0, tiled=True)


def gather(x, axis):
    return exchange(jnp.broadcast_to(x[None], (SIZES[axis],) + x.shape), axis)


def cut_body(q, k, v, shared, first, second):
    for i, x in enumerate((q, k, v)):
        for z in range(4):
            for out, heads in ((shared, (4,)), (first, (0, 2)), (second, (1, 3))):
                for c, head in enumerate(heads):
                    lanes = slice((5 * z + head) * LANES, (5 * z + head + 1) * LANES)
                    out[4 * c + z, i] = x[:, lanes]


def cut(q, k, v):
    rows = q.shape[0]
    return pl.pallas_call(
        cut_body,
        out_shape=[jax.ShapeDtypeStruct((n, 3, rows, LANES), BF16) for n in (4, 8, 8)],
    )(q, k, v)


def eye(rows):
    return lax.broadcasted_iota(jnp.int32, (rows, LANES), 0) == lax.broadcasted_iota(
        jnp.int32, (rows, LANES), 1
    )


def write_levels(out, at, level):
    rows = level.shape[0]
    lines = []
    for start in range(0, rows, LANES):
        piece = level[start : start + LANES]
        lines.append(jnp.sum(jnp.where(eye(piece.shape[0]), piece, 0.0), axis=0, keepdims=True))
    line = jnp.concatenate(lines, axis=0)
    high = line.astype(BF16).astype(F32)
    middle = (line - high).astype(BF16).astype(F32)
    low = line - high - middle
    spare = jnp.zeros((LEVEL_ROWS - 3 * len(lines), LANES), F32)
    out[at, rows:, :] = jnp.concatenate([high, middle, low, spare], axis=0).astype(BF16)


def read_levels(block, rows):
    n = -(-rows // LANES)
    parts = block[rows:, :].astype(F32)
    return parts[:n] + parts[n : 2 * n] + parts[2 * n : 3 * n]


def column(line, rows):
    pieces = []
    for i, start in enumerate(range(0, rows, LANES)):
        here = min(LANES, rows - start)
        wide = jnp.broadcast_to(line[i : i + 1], (here, LANES))
        pieces.append(jnp.sum(jnp.where(eye(here), wide, 0.0), axis=1, keepdims=True))
    return jnp.concatenate(pieces, axis=0)


def flash_body(rows, q_ref, kv_ref, out, keys, values):
    key_rows = kv_ref.shape[2]
    values[:, HEAD_DIM:] = jnp.ones((4 * key_rows, LANES), BF16)
    for i in range(4):
        part = pl.ds(i * key_rows, key_rows)
        keys[part, :] = kv_ref[i, 0]
        values[part, :HEAD_DIM] = kv_ref[i, 1]

    def block(i, _):
        q = q_ref[i]
        largest = total = None
        for start in range(0, 4 * key_rows, KEY_TILE):
            part = pl.ds(start, min(KEY_TILE, 4 * key_rows - start))
            scores = lax.dot_general(q, keys[part, :], NT, preferred_element_type=F32)
            new = jnp.max(scores, axis=1, keepdims=True)
            if total is not None:
                new = jnp.maximum(largest, new)
            weights = jnp.exp2((scores - new) * SCALE).astype(BF16)
            update = jnp.dot(weights, values[part, :], preferred_element_type=F32)
            if total is None:
                total = update
            else:
                total = total * jnp.exp2((largest - new) * SCALE) + update
            largest = new
        sums = total[:, HEAD_DIM:]
        result = (total[:, :HEAD_DIM] / sums).astype(BF16)
        level = largest * SCALE + jnp.log2(sums)
        for half in range(2):
            part = slice(half * rows, (half + 1) * rows)
            out[2 * i + half, :rows, :] = result[part]
            write_levels(out, 2 * i + half, level[part])
        return 0

    lax.fori_loop(0, 8, block, 0)


def flash(q, kv):
    rows, key_rows = q.shape[1] // 2, kv.shape[2]
    pairs = 16 * rows * 4 * key_rows
    return pl.pallas_call(
        functools.partial(flash_body, rows),
        out_shape=jax.ShapeDtypeStruct((16, rows + LEVEL_ROWS, LANES), BF16),
        scratch_shapes=[
            pltpu.VMEM((4 * key_rows, HEAD_DIM), BF16),
            pltpu.VMEM((4 * key_rows, 2 * HEAD_DIM), BF16),
        ],
        compiler_params=pltpu.CompilerParams(vmem_limit_bytes=40 << 20),
        cost_estimate=pl.CostEstimate(
            flops=8 * pairs * HEAD_DIM, bytes_accessed=4 << 20, transcendentals=pairs
        ),
    )(q, kv)


def merge_blocks(blocks, rows):
    levels = [read_levels(b, rows) for b in blocks]
    top = functools.reduce(jnp.maximum, levels)
    shares = [jnp.exp2(v - top) for v in levels]
    whole = functools.reduce(jnp.add, shares)
    total = 0.0
    for share, b in zip(shares, blocks):
        total = total + column(share / whole, rows) * b[:rows, :].astype(F32)
    return total.astype(BF16)


def merge_own_body(rows, x, out):
    for z in range(2):
        for c in range(2):
            out[z, c] = merge_blocks([x[4 * i + 2 * c + z] for i in range(4)], rows)


def merge_shared_body(rows, x, out):
    for z in range(2):
        out[z] = merge_blocks([x[4 * i + 2 * c + z] for i in range(4) for c in range(2)], rows)


def merge(body, x, shape):
    return pl.pallas_call(
        functools.partial(body, shape[-2]), out_shape=jax.ShapeDtypeStruct(shape, BF16)
    )(x)


def on_device(query_in, key_in, value_in, residual, out_weight, gate_scale):
    own_rows = query_in.shape[0]
    pair = 2 * own_rows
    other_weight = flip(out_weight, "c")
    zh, core = lax.axis_index("zh"), lax.axis_index("c")

    shared, first, second = cut(query_in, key_in, value_in)

    def spread(x, axes):
        got = exchange(x, axes).transpose(1, 0, 2, 3)
        return got.reshape(3, -1, 4, own_rows, LANES)

    def ordered(q):
        ends_first = jnp.concatenate([q[:, 0:1], q[:, 3:4], q[:, 1:3]], axis=1)
        middle_first = jnp.concatenate([q[:, 1:3], q[:, 0:1], q[:, 3:4]], axis=1)
        return jnp.where(zh == 0, ends_first, middle_first).reshape(2, 2 * pair, LANES)

    def attend(q, kv, key_axis, query_axis):
        q = gather(ordered(q), query_axis).reshape(8, 2 * pair, LANES)
        kv = gather(kv.reshape(2, -1, LANES), key_axis)
        return exchange(flash(q, kv), (query_axis, "c", "zl"))

    got = spread(first, CZ)
    second, got = lax.optimization_barrier((second, got))
    got_second = spread(second, CZ)
    shared, got_second = lax.optimization_barrier((shared, got_second))
    got_shared = spread(shared, Z)

    first = merge(merge_own_body, attend(got[0], got[1:], "y", "x"), (2, 2, pair, LANES))
    second = attend(got_second[0], got_second[1:], "x", "y")
    second = merge(merge_own_body, second, (2, 2, pair, LANES))
    q, q_there = got_shared[0], flip(got_shared[0], "c")
    q = jnp.concatenate(
        [jnp.where(core == 0, q, q_there), jnp.where(core == 0, q_there, q)], axis=0
    )
    shared = merge(merge_shared_body, attend(q, got_shared[1:], "y", "x"), (2, pair, LANES))

    groups = [
        jnp.concatenate([first[z, 0], second[z, 0], first[z, 1], second[z, 1], shared[z]], axis=1)
        for z in range(2)
    ]
    for_own = jnp.where(core == 0, groups[0], groups[1])
    for_other = jnp.where(core == 0, groups[1], groups[0])
    width = out_weight.shape[1] // 2
    outs = []
    for part in range(2):
        columns = slice(part * width, (part + 1) * width)
        partial = jnp.dot(
            for_own, out_weight[:, columns], preferred_element_type=F32
        ) + jnp.dot(for_other, other_weight[:, columns], preferred_element_type=F32)
        low, high = partial[:own_rows], partial[own_rows:]
        theirs = jnp.where(zh == 0, high, low).astype(BF16)
        ours = jnp.where(zh == 0, low, high)
        projected = ours + flip(theirs, "zh", "zl").astype(F32)
        outs.append(
            (residual[:, columns].astype(F32) + gate_scale[columns] * projected).astype(BF16)
        )
    return jnp.concatenate(outs, axis=1)


def solution(mesh):
    fine = Mesh(mesh.devices.reshape(tuple(SIZES.values())), ALL)
    tokens = P(ALL, None)
    return jax.shard_map(
        on_device,
        mesh=fine,
        in_specs=(tokens, tokens, tokens, tokens, P(("zh", "c"), None), P()),
        out_specs=tokens,
        check_vma=False,
    )
```

```python
import functools

import jax
import jax.numpy as jnp
from jax import lax
from jax.experimental import pallas as pl
from jax.experimental.pallas import tpu as pltpu
from jax.sharding import Mesh
from jax.sharding import PartitionSpec as P

HEAD_DIM = 128
LANES = 128
SCALE = HEAD_DIM**-0.5 * 1.4426950408889634
ALL = ("zh", "c", "y", "zl", "x")
SIZES = {"zh": 2, "c": 2, "y": 4, "zl": 2, "x": 4}
Z = ("zh", "zl")
CZ = ("c", "zh", "zl")
KEY_TILE = 256
LEVEL_ROWS = 16
F32 = jnp.float32
BF16 = jnp.bfloat16
NT = (((1,), (1,)), ((), ()))


def flip(x, *names):
    total = 2 ** len(names)
    return lax.ppermute(x, names, [(i, total - 1 - i) for i in range(total)])


def exchange(x, axes):
    return lax.all_to_all(x, axes, split_axis=0, concat_axis=0, tiled=True)


def shift(x, axis, by):
    n = SIZES[axis]
    return lax.ppermute(x, axis, [(i, (i + by) % n) for i in range(n)])


def gather(x, axis):
    left, right = shift(x, axis, 1), shift(x, axis, -1)
    return [x, left, right, shift(left[0], axis, 1), shift(right[1], axis, -1)]


def cut_body(q, k, v, shared, first, second):
    for i, x in enumerate((q, k, v)):
        for z in range(4):
            for out, heads in ((shared, (4,)), (first, (0, 1)), (second, (2, 3))):
                for c, head in enumerate(heads):
                    lanes = slice((5 * z + head) * LANES, (5 * z + head + 1) * LANES)
                    out[4 * c + z, i] = x[:, lanes]


def cut(q, k, v):
    rows = q.shape[0]
    return pl.pallas_call(
        cut_body,
        out_shape=[jax.ShapeDtypeStruct((n, 3, rows, LANES), BF16) for n in (4, 8, 8)],
    )(q, k, v)


def eye(rows):
    return lax.broadcasted_iota(jnp.int32, (rows, LANES), 0) == lax.broadcasted_iota(
        jnp.int32, (rows, LANES), 1
    )


def write_levels(out, at, level):
    rows = level.shape[0]
    lines = []
    for start in range(0, rows, LANES):
        piece = level[start : start + LANES]
        lines.append(jnp.sum(jnp.where(eye(piece.shape[0]), piece, 0.0), axis=0, keepdims=True))
    line = jnp.concatenate(lines, axis=0)
    high = line.astype(BF16).astype(F32)
    middle = (line - high).astype(BF16).astype(F32)
    low = line - high - middle
    spare = jnp.zeros((LEVEL_ROWS - 3 * len(lines), LANES), F32)
    out[at, rows:, :] = jnp.concatenate([high, middle, low, spare], axis=0).astype(BF16)


def read_levels(block, rows):
    n = -(-rows // LANES)
    parts = block[rows:, :].astype(F32)
    return parts[:n] + parts[n : 2 * n] + parts[2 * n : 3 * n]


def flash_body(rows, query_axis, parts, *refs):
    q_own, q_left, q_right, *q_far = refs[:5]
    kv_own, kv_left, kv_right, *kv_far = refs[5:10]
    out, queries, keys, values = refs[10:]
    me = lax.axis_index(query_axis)
    values[:, HEAD_DIM:] = jnp.ones((values.shape[0], LANES), BF16)
    half_rows = 2 * rows
    first_key = 0
    for part, key_rows in enumerate(parts):
        these = slice(first_key, first_key + key_rows)
        first_key += key_rows
        for i, ref in enumerate((kv_own, kv_left, kv_right)):
            to = slice(i * key_rows, (i + 1) * key_rows)
            keys[to, :] = ref[0, these, :]
            values[to, :HEAD_DIM] = ref[1, these, :]
        to = slice(3 * key_rows, 4 * key_rows)
        keys[to, :] = kv_far[0][these, :]
        values[to, :HEAD_DIM] = kv_far[1][these, :]
        for half in range(2):
            for place, ref in ((0, q_own), (1, q_right), (3, q_left)):
                if len(parts) == 1:
                    queries[2 * place + half] = ref[half]
                else:
                    queries[2 * place + half] = ref[part, half * half_rows : (half + 1) * half_rows, :]
            if len(parts) == 1:
                queries[4 + half] = q_far[half][...]
            else:
                queries[4 + half] = q_far[part][half * half_rows : (half + 1) * half_rows, :]

        def block(i, _):
            q = queries[i]
            largest = total = None
            for start in range(0, 4 * key_rows, KEY_TILE):
                tile = pl.ds(start, min(KEY_TILE, 4 * key_rows - start))
                scores = lax.dot_general(q, keys[tile, :], NT, preferred_element_type=F32)
                new = jnp.max(scores, axis=1, keepdims=True)
                if total is not None:
                    new = jnp.maximum(largest, new)
                weights = jnp.exp2((scores - new) * SCALE).astype(BF16)
                update = jnp.dot(weights, values[tile, :], preferred_element_type=F32)
                if total is None:
                    total = update
                else:
                    total = total * jnp.exp2((largest - new) * SCALE) + update
                largest = new
            sums = total[:, HEAD_DIM:]
            result = (total[:, :HEAD_DIM] / sums).astype(BF16)
            level = largest * SCALE + jnp.log2(sums)
            place = lax.rem(me + lax.div(i, 2), 4)
            for half in range(2):
                at = 4 * place + 2 * lax.rem(i, 2) + half
                here = slice(half * rows, (half + 1) * rows)
                out[at, part, :rows, :] = result[here]
                write_levels(out.at[at], part, level[here])
            return 0

        lax.fori_loop(0, 8, block, 0)


def flash(queries, kvs, rows, query_axis, parts):
    pairs = 16 * rows * 4 * sum(parts)
    return pl.pallas_call(
        functools.partial(flash_body, rows, query_axis, parts),
        out_shape=jax.ShapeDtypeStruct((16, len(parts), rows + LEVEL_ROWS, LANES), BF16),
        scratch_shapes=[
            pltpu.VMEM((8, 2 * rows, HEAD_DIM), BF16),
            pltpu.VMEM((4 * max(parts), HEAD_DIM), BF16),
            pltpu.VMEM((4 * max(parts), 2 * HEAD_DIM), BF16),
        ],
        compiler_params=pltpu.CompilerParams(vmem_limit_bytes=40 << 20),
        cost_estimate=pl.CostEstimate(
            flops=8 * pairs * HEAD_DIM, bytes_accessed=4 << 20, transcendentals=pairs
        ),
    )(*queries, *kvs)


def merge_blocks(blocks, rows):
    levels = [read_levels(b, rows) for b in blocks]
    top = functools.reduce(jnp.maximum, levels)
    shares = [jnp.exp2(v - top) for v in levels]
    whole = functools.reduce(jnp.add, shares)
    shares = [share / whole for share in shares]
    pieces = []
    for i, start in enumerate(range(0, rows, LANES)):
        here = min(LANES, rows - start)
        total = 0.0
        for share, b in zip(shares, blocks):
            wide = jnp.broadcast_to(share[i : i + 1, :here], (here, here))
            diagonal = jnp.where(eye(here)[:, :here], wide, 0.0).astype(BF16)
            total = total + jnp.dot(
                diagonal, b[start : start + here, :], preferred_element_type=F32
            )
        pieces.append(total.astype(BF16))
    return jnp.concatenate(pieces, axis=0)


def merge_body(rows, x, out):
    for z in range(2):
        for c in range(2):
            value = merge_blocks([x[4 * i + 2 * c + z, 0] for i in range(4)], rows)
            out[z, :, c * LANES : (c + 1) * LANES] = value
        if x.shape[1] > 1:
            both = [x[4 * i + 2 * c + z, 1] for i in range(4) for c in range(2)]
            out[z, :, 2 * LANES :] = merge_blocks(both, rows)


def merge(x):
    rows, heads = x.shape[2] - LEVEL_ROWS, x.shape[1] + 1
    return pl.pallas_call(
        functools.partial(merge_body, rows),
        out_shape=jax.ShapeDtypeStruct((2, rows, heads * LANES), BF16),
    )(x)


def on_device(query_in, key_in, value_in, residual, out_weight, gate_scale):
    own_rows = query_in.shape[0]
    pair = 2 * own_rows
    other_weight = flip(out_weight, "c")
    zh, core = lax.axis_index("zh"), lax.axis_index("c")

    shared, first, second = cut(query_in, key_in, value_in)

    def spread(x, axes):
        got = exchange(x, axes).transpose(1, 0, 2, 3)
        return got.reshape(3, -1, 4, own_rows, LANES)

    def ordered(q):
        ends_first = jnp.concatenate([q[:, 0:1], q[:, 3:4], q[:, 1:3]], axis=1)
        middle_first = jnp.concatenate([q[:, 1:3], q[:, 0:1], q[:, 3:4]], axis=1)
        return jnp.where(zh == 0, ends_first, middle_first).reshape(2, 2 * pair, LANES)

    def attend(q, kv, parts, key_axis, query_axis):
        out = flash(gather(q, query_axis), gather(kv, key_axis), pair, query_axis, parts)
        return merge(exchange(out, (query_axis, "c", "zl")))

    got = spread(first, CZ)
    second, shared, got = lax.optimization_barrier((second, shared, got))
    got_second = spread(second, CZ)
    shared, got_second = lax.optimization_barrier((shared, got_second))
    got_shared = spread(shared, Z)

    rows = 8 * own_rows
    first = attend(ordered(got[0]), got[1:].reshape(2, rows, LANES), (rows,), "y", "x")
    q_here, q_there = got_shared[0], flip(got_shared[0], "c")
    q_shared = jnp.concatenate(
        [jnp.where(core == 0, q_here, q_there), jnp.where(core == 0, q_there, q_here)], axis=0
    )
    q = jnp.stack([ordered(x).reshape(rows, LANES) for x in (got_second[0], q_shared)])
    kv = jnp.concatenate(
        [x[1:].reshape(2, -1, LANES) for x in (got_second, got_shared)], axis=1
    )
    second = attend(q, kv, (rows, rows // 2), "x", "y")

    cut_at = first.shape[2]
    width = out_weight.shape[1] // 2
    outs = []
    for part in range(2):
        columns = slice(part * width, (part + 1) * width)
        partial = 0.0
        for x, inner in ((first, slice(0, cut_at)), (second, slice(cut_at, None))):
            for_own = jnp.where(core == 0, x[0], x[1])
            for_other = jnp.where(core == 0, x[1], x[0])
            for side, weight in ((for_own, out_weight), (for_other, other_weight)):
                partial += jnp.dot(side, weight[inner, columns], preferred_element_type=F32)
        low, high = partial[:own_rows], partial[own_rows:]
        theirs = jnp.where(zh == 0, high, low).astype(BF16)
        ours = jnp.where(zh == 0, low, high)
        projected = ours + flip(theirs, "zh", "zl").astype(F32)
        outs.append(
            (residual[:, columns].astype(F32) + gate_scale[columns] * projected).astype(BF16)
        )
    return jnp.concatenate(outs, axis=1)


def solution(mesh):
    fine = Mesh(mesh.devices.reshape(tuple(SIZES.values())), ALL)
    tokens = P(ALL, None)
    return jax.shard_map(
        on_device,
        mesh=fine,
        in_specs=(tokens, tokens, tokens, tokens, P(("zh", "c"), None), P()),
        out_specs=tokens,
        check_vma=False,
    )
```

```python
import functools

import jax
import jax.numpy as jnp
from jax import lax
from jax.experimental import pallas as pl
from jax.experimental.pallas import tpu as pltpu
from jax.sharding import Mesh
from jax.sharding import PartitionSpec as P

HEAD_DIM = 128
LANES = 128
SCALE = HEAD_DIM**-0.5 * 1.4426950408889634
ALL = ("zh", "c", "y", "zl", "x")
SIZES = {"zh": 2, "c": 2, "y": 4, "zl": 2, "x": 4}
CZ = ("c", "zh", "zl")
KEY_TILE = 256
LEVEL_ROWS = 16
F32 = jnp.float32
BF16 = jnp.bfloat16
NT = (((1,), (1,)), ((), ()))


def flip(x, *names):
    total = 2 ** len(names)
    return lax.ppermute(x, names, [(i, total - 1 - i) for i in range(total)])


def exchange(x, axes):
    return lax.all_to_all(x, axes, split_axis=0, concat_axis=0, tiled=True)


def after(arrays, others):
    return pl.pallas_call(
        lambda *refs: None,
        out_shape=[jax.ShapeDtypeStruct(x.shape, x.dtype) for x in arrays],
        in_specs=[pl.BlockSpec(memory_space=pl.ANY)] * (len(arrays) + len(others)),
        out_specs=[pl.BlockSpec(memory_space=pl.ANY)] * len(arrays),
        input_output_aliases={i: i for i in range(len(arrays))},
        cost_estimate=pl.CostEstimate(flops=0, bytes_accessed=0, transcendentals=0),
    )(*arrays, *others)


def shift(x, axis, by):
    n = SIZES[axis]
    return lax.ppermute(x, axis, [(i, (i + by) % n) for i in range(n)])


def neighbours(x, axis):
    return [shift(x, axis, 1), shift(x, axis, -1)]


def far(halves, axis):
    return [shift(halves[0], axis, 1), shift(halves[1], axis, -1)]


def cut_body(heads_of, q, k, v, out):
    for i, x in enumerate((q, k, v)):
        for z in range(4):
            for c in range(2):
                for part, heads in enumerate(heads_of):
                    first = (5 * z + heads[c]) * LANES
                    out[4 * c + z, 3 * part + i] = x[:, first : first + LANES]


def cut(q, k, v, heads_of):
    return pl.pallas_call(
        functools.partial(cut_body, heads_of),
        out_shape=jax.ShapeDtypeStruct((8, 3 * len(heads_of), q.shape[0], LANES), BF16),
    )(q, k, v)


def eye(rows):
    return lax.broadcasted_iota(jnp.int32, (rows, LANES), 0) == lax.broadcasted_iota(
        jnp.int32, (rows, LANES), 1
    )


def write_levels(out, at, level):
    rows = level.shape[0]
    lines = []
    for start in range(0, rows, LANES):
        piece = level[start : start + LANES]
        lines.append(jnp.sum(jnp.where(eye(piece.shape[0]), piece, 0.0), axis=0, keepdims=True))
    line = jnp.concatenate(lines, axis=0)
    high = line.astype(BF16).astype(F32)
    middle = (line - high).astype(BF16).astype(F32)
    low = line - high - middle
    spare = jnp.zeros((LEVEL_ROWS - 3 * len(lines), LANES), F32)
    out[at, rows:, :] = jnp.concatenate([high, middle, low, spare], axis=0).astype(BF16)


def read_levels(block, rows):
    n = -(-rows // LANES)
    parts = block[rows:, :].astype(F32)
    return parts[:n] + parts[n : 2 * n] + parts[2 * n : 3 * n]


def flash_body(rows, query_axis, first_key, part, units, based, *refs):
    q_own, q_left, q_right, *q_far = refs[:5]
    kv_own, kv_left, kv_right, *kv_far = refs[5:10]
    base = refs[10] if based else None
    out, keys, values = refs[-3:]
    me = lax.axis_index(query_axis)
    key_rows = keys.shape[0] // 4
    these = slice(first_key, first_key + key_rows)
    values[:, HEAD_DIM:] = jnp.ones((4 * key_rows, LANES), BF16)
    for i, ref in enumerate((kv_own, kv_left, kv_right)):
        to = slice(i * key_rows, (i + 1) * key_rows)
        keys[to, :] = ref[0, these, :]
        values[to, :HEAD_DIM] = ref[1, these, :]
    to = slice(3 * key_rows, 4 * key_rows)
    keys[to, :] = kv_far[0][these, :]
    values[to, :HEAD_DIM] = kv_far[1][these, :]

    def place(unit):
        return 4 * lax.rem(me + unit, 4)

    def query(unit):
        if unit == 2:
            if part is None:
                return jnp.concatenate([q_far[0][...], q_far[1][...]], axis=0)
            return q_far[part][...]
        ref = {0: q_own, 1: q_right, 3: q_left}[unit]
        return ref[...].reshape(4 * rows, HEAD_DIM) if part is None else ref[part]

    if based:
        for unit in range(4):
            if unit not in units:
                for k in range(4):
                    out[place(unit) + k] = base[place(unit) + k]

    for unit in units:
        q = query(unit)
        largest = total = None
        for start in range(0, 4 * key_rows, KEY_TILE):
            tile = pl.ds(start, min(KEY_TILE, 4 * key_rows - start))
            scores = lax.dot_general(q, keys[tile, :], NT, preferred_element_type=F32)
            new = jnp.max(scores, axis=1, keepdims=True)
            if total is not None:
                new = jnp.maximum(largest, new)
            weights = jnp.exp2((scores - new) * SCALE).astype(BF16)
            update = jnp.dot(weights, values[tile, :], preferred_element_type=F32)
            if total is None:
                total = update
            else:
                total = total * jnp.exp2((largest - new) * SCALE) + update
            largest = new
        sums = total[:, HEAD_DIM:]
        result = (total[:, :HEAD_DIM] / sums).astype(BF16)
        level = largest * SCALE + jnp.log2(sums)
        for k in range(4):
            here = slice(k * rows, (k + 1) * rows)
            out[place(unit) + k, :rows, :] = result[here]
            write_levels(out, place(unit) + k, level[here])


def flash(queries, kvs, rows, query_axis, keys_at, part, units, base=None):
    first_key, key_rows = keys_at
    pairs = 4 * rows * len(units) * 4 * key_rows
    extra = () if base is None else (base,)
    return pl.pallas_call(
        functools.partial(flash_body, rows, query_axis, first_key, part, units, base is not None),
        out_shape=jax.ShapeDtypeStruct((16, rows + LEVEL_ROWS, LANES), BF16),
        scratch_shapes=[
            pltpu.VMEM((4 * key_rows, HEAD_DIM), BF16),
            pltpu.VMEM((4 * key_rows, 2 * HEAD_DIM), BF16),
        ],
        compiler_params=pltpu.CompilerParams(vmem_limit_bytes=40 << 20),
        cost_estimate=pl.CostEstimate(
            flops=8 * pairs * HEAD_DIM, bytes_accessed=4 << 20, transcendentals=pairs
        ),
    )(*queries, *kvs, *extra)


def merge_blocks(blocks, rows):
    levels = [read_levels(b, rows) for b in blocks]
    top = functools.reduce(jnp.maximum, levels)
    shares = [jnp.exp2(v - top) for v in levels]
    whole = functools.reduce(jnp.add, shares)
    shares = [share / whole for share in shares]
    pieces = []
    for i, start in enumerate(range(0, rows, LANES)):
        here = min(LANES, rows - start)
        total = 0.0
        for share, b in zip(shares, blocks):
            wide = jnp.broadcast_to(share[i : i + 1, :here], (here, here))
            diagonal = jnp.where(eye(here)[:, :here], wide, 0.0).astype(BF16)
            total = total + jnp.dot(
                diagonal, b[start : start + here, :], preferred_element_type=F32
            )
        pieces.append(total.astype(BF16))
    return jnp.concatenate(pieces, axis=0)


def merge_body(rows, shared, x, out):
    for z in range(2):
        if shared:
            both = [x[4 * i + 2 * c + z] for i in range(4) for c in range(2)]
            out[z] = merge_blocks(both, rows)
        else:
            for c in range(2):
                value = merge_blocks([x[4 * i + 2 * c + z] for i in range(4)], rows)
                out[z, :, c * LANES : (c + 1) * LANES] = value


def merge(x, shared):
    rows = x.shape[1] - LEVEL_ROWS
    return pl.pallas_call(
        functools.partial(merge_body, rows, shared),
        out_shape=jax.ShapeDtypeStruct((2, rows, LANES if shared else 2 * LANES), BF16),
    )(x)


def project_body(first, middle, last, own, other, theirs, ours):
    core, zh = lax.axis_index("c"), lax.axis_index("zh")
    rows = ours.shape[0]

    def product(group, weight):
        features = jnp.concatenate([x[group] for x in (first, middle, last)], axis=1)
        return jnp.dot(features, weight[...], preferred_element_type=F32)

    partial = product(core, own) + product(1 - core, other)
    low, high = partial[:rows], partial[rows:]
    theirs[...] = jnp.where(zh == 0, high, low).astype(BF16)
    ours[...] = jnp.where(zh == 0, low, high)


def project(parts, own, other, rows):
    inner, width = own.shape
    block = 512
    fixed = [pl.BlockSpec(x.shape, lambda i: (0, 0, 0)) for x in parts]
    return pl.pallas_call(
        project_body,
        grid=(width // block,),
        in_specs=fixed + [pl.BlockSpec((inner, block), lambda i: (0, i))] * 2,
        out_specs=[pl.BlockSpec((rows, block), lambda i: (0, i))] * 2,
        out_shape=[
            jax.ShapeDtypeStruct((rows, width), BF16),
            jax.ShapeDtypeStruct((rows, width), F32),
        ],
        cost_estimate=pl.CostEstimate(
            flops=8 * rows * inner * width, bytes_accessed=4 * inner * width, transcendentals=0
        ),
    )(*parts, own, other)


def on_device(query_in, key_in, value_in, residual, out_weight, gate_scale):
    own_rows = query_in.shape[0]
    pair, rows = 2 * own_rows, 8 * own_rows
    other_weight = flip(out_weight, "c")
    zh, core = lax.axis_index("zh"), lax.axis_index("c")

    def spread(heads_of):
        got = exchange(cut(query_in, key_in, value_in, heads_of), CZ)
        return got.transpose(1, 0, 2, 3).reshape(-1, 2, 4, own_rows, LANES)

    got, got_second = spread(((0, 1),)), spread(((3, 4), (2, 2)))

    def ordered(q):
        ends_first = jnp.concatenate([q[:, 0:1], q[:, 3:4], q[:, 1:3]], axis=1)
        middle_first = jnp.concatenate([q[:, 1:3], q[:, 0:1], q[:, 3:4]], axis=1)
        return jnp.where(zh == 0, ends_first, middle_first).reshape(2, 2 * pair, LANES)

    q, kv = ordered(got[0]), got[1:].reshape(2, rows, LANES)
    kv_near, q_near = neighbours(kv, "y"), neighbours(q, "x")
    halves = [kv_near[0][0], kv_near[1][1], q_near[0][0], q_near[1][1]]
    halves = after(halves, kv_near + q_near)
    kv_far, q_far = far(halves[:2], "y"), far(halves[2:], "x")

    q_second = jnp.stack([ordered(got_second[i]).reshape(rows, LANES) for i in (0, 3)])
    shared = got_second[4:]
    shared = jnp.where(core == 0, shared[:, 0], shared[:, 1]).reshape(2, 4 * own_rows, LANES)
    kv_second = jnp.concatenate([got_second[1:3].reshape(2, rows, LANES), shared], axis=1)
    q_second, kv_second = after([q_second, kv_second], kv_far + q_far)
    kv_near_second, q_near_second = neighbours(kv_second, "x"), neighbours(q_second, "y")

    stage = ([q] + q_near + q_far, [kv] + kv_near + kv_far, pair, "x", (0, rows), None)
    out = flash(*stage, (1, 2, 3))

    halves = [kv_near_second[0][0], kv_near_second[1][1], q_near_second[0][0], q_near_second[1][1]]
    halves = after(halves, kv_near_second + q_near_second + [out])
    kv_far, q_far = far(halves[:2], "x"), far(halves[2:], "y")

    first = exchange(flash(*stage, (0,), out), ("x", "c", "zl"))
    stage = ([q_second] + q_near_second + q_far, [kv_second] + kv_near_second + kv_far, pair, "y")
    every = (0, 1, 2, 3)
    middle = exchange(flash(*stage, (rows, rows // 2), 1, every), ("y", "c", "zl"))
    last = exchange(flash(*stage, (0, rows), 0, every), ("y", "c", "zl"))

    parts = [merge(first, False), merge(middle, True), merge(last, False)]
    theirs, ours = project(parts, out_weight, other_weight, own_rows)
    projected = ours + flip(theirs, "zh", "zl").astype(F32)
    return (residual.astype(F32) + gate_scale * projected).astype(BF16)


def solution(mesh):
    fine = Mesh(mesh.devices.reshape(tuple(SIZES.values())), ALL)
    tokens = P(ALL, None)
    return jax.shard_map(
        on_device,
        mesh=fine,
        in_specs=(tokens, tokens, tokens, tokens, P(("zh", "c"), None), P()),
        out_specs=tokens,
        check_vma=False,
    )
```

```python
import functools

import jax
import jax.numpy as jnp
from jax import lax
from jax.experimental import pallas as pl
from jax.experimental.pallas import tpu as pltpu
from jax.sharding import Mesh
from jax.sharding import PartitionSpec as P

HEAD_DIM = 128
LANES = 128
SCALE = HEAD_DIM**-0.5 * 1.4426950408889634
ALL = ("zh", "c", "y", "zl", "x")
SIZES = {"zh": 2, "c": 2, "y": 4, "zl": 2, "x": 4}
CZ = ("c", "zh", "zl")
KEY_TILE = 256
LEVEL_ROWS = 16
VMEM_BYTES = 20 << 20
F32 = jnp.float32
BF16 = jnp.bfloat16
NT = (((1,), (1,)), ((), ()))


def flip(x, *names):
    total = 2 ** len(names)
    return lax.ppermute(x, names, [(i, total - 1 - i) for i in range(total)])


def exchange(x, axes):
    return lax.all_to_all(x, axes, split_axis=0, concat_axis=0, tiled=True)


def shift(x, axis, by):
    n = SIZES[axis]
    return lax.ppermute(x, axis, [(i, (i + by) % n) for i in range(n)])


def neighbours(x, axis):
    return [shift(x, axis, 1), shift(x, axis, -1)]


def far(halves, axis):
    return [shift(halves[0], axis, 1), shift(halves[1], axis, -1)]


def halves_body(n_extra, *refs):
    kv_left, kv_right, q_left, q_right = refs[:4]
    outs = refs[4 + n_extra :]
    outs[0][...], outs[1][...] = kv_left[0], kv_right[1]
    outs[2][...], outs[3][...] = q_left[0], q_right[1]
    if len(outs) > 4:
        outs[4][...] = refs[4][...]


def halves(kv_near, q_near, extra, hand_on=False):
    like = [kv_near[0][0], kv_near[1][1], q_near[0][0], q_near[1][1]] + ([extra] if hand_on else [])
    return pl.pallas_call(
        functools.partial(halves_body, 1),
        out_shape=[jax.ShapeDtypeStruct(x.shape, x.dtype) for x in like],
        compiler_params=pltpu.CompilerParams(vmem_limit_bytes=VMEM_BYTES),
    )(*kv_near, *q_near, extra)


def second_body(got, first_far, second_far, q, kv):
    core = lax.axis_index("c")
    for i in range(8):
        q[0, i], q[1, i] = got[i, 0], got[i, 3]
        kv[0, i], kv[1, i] = got[i, 1], got[i, 2]
    for z in range(4):
        kv[0, 8 + z], kv[1, 8 + z] = got[4 * core + z, 4], got[4 * core + z, 5]


def second_stage(got, earlier):
    rows = got.shape[2]
    shapes = [(2, 8, rows, LANES), (2, 12, rows, LANES)]
    q, kv = pl.pallas_call(
        second_body,
        out_shape=[jax.ShapeDtypeStruct(x, BF16) for x in shapes],
        compiler_params=pltpu.CompilerParams(vmem_limit_bytes=VMEM_BYTES),
    )(got, *earlier)
    return q.reshape(2, 8 * rows, LANES), kv.reshape(2, 12 * rows, LANES)


def cut_body(heads_of, q, k, v, *outs):
    for out, parts in zip(outs, heads_of):
        for part, heads in enumerate(parts):
            for c in range(2):
                for z in range(4):
                    first = (5 * z + heads[c]) * LANES
                    for i, x in enumerate((q, k, v)):
                        out[4 * c + z, 3 * part + i] = x[:, first : first + LANES]


def cut(q, k, v, heads_of):
    return pl.pallas_call(
        functools.partial(cut_body, heads_of),
        out_shape=[
            jax.ShapeDtypeStruct((8, 3 * len(parts), q.shape[0], LANES), BF16)
            for parts in heads_of
        ],
    )(q, k, v)


def eye(rows):
    return lax.broadcasted_iota(jnp.int32, (rows, LANES), 0) == lax.broadcasted_iota(
        jnp.int32, (rows, LANES), 1
    )


def write_block(out, at, part, result, level):
    rows = result.shape[0]
    padding = jnp.zeros((out.shape[2] - LEVEL_ROWS - rows, LANES), F32)
    line = jnp.sum(jnp.where(eye(rows), level, 0.0), axis=0, keepdims=True)
    high = line.astype(BF16).astype(F32)
    middle = (line - high).astype(BF16).astype(F32)
    spare = jnp.zeros((LEVEL_ROWS - 3, LANES), F32)
    block = [result, padding, high, middle, line - high - middle, spare]
    out[at, part] = jnp.concatenate(block, axis=0).astype(BF16)


def read_level(block):
    parts = block[-LEVEL_ROWS:, :].astype(F32)
    return parts[0:1] + parts[1:2] + parts[2:3]


def flash_body(rows, query_axis, first_key, part, units, based, out_part, *refs):
    token, refs = refs[-3], refs[:-3] + refs[-2:]
    token[...] = jnp.zeros_like(token)
    q_own, q_left, q_right, *q_far = refs[:5]
    kv_own, kv_left, kv_right, *kv_far = refs[5:10]
    base = refs[10]
    out, keys, values = refs[-3:]
    me = lax.axis_index(query_axis)
    key_rows = keys.shape[0] // 4
    these = slice(first_key, first_key + key_rows)
    values[:, HEAD_DIM:] = jnp.ones((4 * key_rows, LANES), BF16)
    for i, ref in enumerate((kv_own, kv_left, kv_right)):
        to = slice(i * key_rows, (i + 1) * key_rows)
        keys[to, :] = ref[0, these, :]
        values[to, :HEAD_DIM] = ref[1, these, :]
    to = slice(3 * key_rows, 4 * key_rows)
    keys[to, :] = kv_far[0][these, :]
    values[to, :HEAD_DIM] = kv_far[1][these, :]

    def place(unit):
        return 8 * lax.rem(me + unit, 4)

    def query(unit):
        if unit == 2:
            if part is None:
                return jnp.concatenate([q_far[0][...], q_far[1][...]], axis=0)
            return q_far[part][...]
        ref = {0: q_own, 1: q_right, 3: q_left}[unit]
        return ref[...].reshape(8 * rows, HEAD_DIM) if part is None else ref[part]

    if based and based[0]:
        for unit in range(4):
            if unit not in units or out_part > 0:
                for k in range(8):
                    out[place(unit) + k, 0] = base[place(unit) + k, 0]

    for unit in units:
        q = query(unit)
        largest = total = None
        for start in range(0, 4 * key_rows, KEY_TILE):
            tile = pl.ds(start, min(KEY_TILE, 4 * key_rows - start))
            scores = lax.dot_general(q, keys[tile, :], NT, preferred_element_type=F32)
            new = jnp.max(scores, axis=1, keepdims=True)
            if total is not None:
                new = jnp.maximum(largest, new)
            weights = jnp.exp2((scores - new) * SCALE).astype(BF16)
            update = jnp.dot(weights, values[tile, :], preferred_element_type=F32)
            if total is None:
                total = update
            else:
                total = total * jnp.exp2((largest - new) * SCALE) + update
            largest = new
        sums = total[:, HEAD_DIM:]
        level = largest * SCALE + jnp.log2(sums)
        for k in range(8):
            here = slice(k * rows, (k + 1) * rows)
            write_block(out, place(unit) + k, out_part, total[here, :HEAD_DIM] / sums[here], level[here])


def flash(queries, kvs, rows, query_axis, keys_at, part, units, base=None, out_part=0, token=None):
    first_key, key_rows = keys_at
    pairs = 8 * rows * len(units) * 4 * key_rows
    extra = [x for x in (base, token) if x is not None]
    block_rows = -(-rows // 16) * 16 + LEVEL_ROWS
    return pl.pallas_call(
        functools.partial(
            flash_body, rows, query_axis, first_key, part, units, (base is not None,), out_part
        ),
        out_shape=[
            jax.ShapeDtypeStruct((32, out_part + 1, block_rows, LANES), BF16),
            jax.ShapeDtypeStruct((8, LANES), F32),
        ],
        scratch_shapes=[
            pltpu.VMEM((4 * key_rows, HEAD_DIM), BF16),
            pltpu.VMEM((4 * key_rows, 2 * HEAD_DIM), BF16),
        ],
        compiler_params=pltpu.CompilerParams(vmem_limit_bytes=VMEM_BYTES),
        cost_estimate=pl.CostEstimate(
            flops=8 * pairs * HEAD_DIM, bytes_accessed=4 << 20, transcendentals=pairs
        ),
    )(*queries, *kvs, *extra)


def merge_blocks(blocks, rows):
    levels = [read_level(b) for b in blocks]
    top = functools.reduce(jnp.maximum, levels)
    shares = [jnp.exp2(v - top) for v in levels]
    whole = functools.reduce(jnp.add, shares)
    total = 0.0
    for share, b in zip(shares, blocks):
        wide = jnp.broadcast_to((share / whole)[:, :rows], (rows, rows))
        diagonal = jnp.where(eye(rows)[:, :rows], wide, 0.0).astype(BF16)
        total = total + jnp.dot(diagonal, b[:rows, :], preferred_element_type=F32)
    return total.astype(BF16)


def merge_body(x, out):
    rows = out.shape[1]
    for z in range(4):
        for c in range(2):
            value = merge_blocks([x[8 * i + 4 * c + z, 0] for i in range(4)], rows)
            out[z, :, c * LANES : (c + 1) * LANES] = value
        if x.shape[1] > 1:
            both = [x[8 * i + 4 * c + z, 1] for i in range(4) for c in range(2)]
            out[z, :, 2 * LANES :] = merge_blocks(both, rows)


def merge(x, rows):
    return pl.pallas_call(
        merge_body, out_shape=jax.ShapeDtypeStruct((4, rows, (x.shape[1] + 1) * LANES), BF16)
    )(x)


def products(features, weights):
    core, zh = lax.axis_index("c"), lax.axis_index("zh")
    groups = (2 * zh + core, 2 * zh + 1 - core, 2 - 2 * zh, 3 - 2 * zh)
    total = 0.0
    for group, pieces in zip(groups, weights):
        x, at = features[group], 0
        for piece in pieces:
            w = piece[...].reshape(piece.shape[-2:])
            total += jnp.dot(x[:, at : at + w.shape[0]], w, preferred_element_type=F32)
            at += w.shape[0]
    return total


def early_body(features, *refs):
    weights, out = refs[:-1], refs[-1]
    out[...] = products(features, [weights[2 * i : 2 * i + 2] for i in range(4)])


def late_body(features, *refs):
    weights, (early, residual, gate, out) = refs[:4], refs[4:]
    total = early[...] + products(features, [[w] for w in weights])
    out[...] = (residual[...].astype(F32) + gate[...] * total).astype(BF16)


def weight_specs(row_blocks, block):
    specs = []
    for far_group in (None, None, 0, 1):
        for rows, at in row_blocks:
            if far_group is None:
                specs.append(pl.BlockSpec((rows, block), lambda i, at=at: (at, i)))
            else:
                specs.append(
                    pl.BlockSpec((1, rows, block), lambda i, at=at, g=far_group: (g, at, i))
                )
    return specs


def project(body, features, row_blocks, weights, extra, out_type):
    rows, width, block = features.shape[1], weights[0].shape[1], 512
    operands, specs = [], weight_specs(row_blocks, block)
    for w in weights:
        operands += [w] * len(row_blocks)
    for x in extra:
        specs.append(pl.BlockSpec((x.shape[0], block), lambda i: (0, i)))
    depth = 4 * features.shape[2]
    return pl.pallas_call(
        body,
        grid=(width // block,),
        in_specs=[pl.BlockSpec(features.shape, lambda i: (0, 0, 0))] + specs,
        out_specs=pl.BlockSpec((rows, block), lambda i: (0, i)),
        out_shape=jax.ShapeDtypeStruct((rows, width), out_type),
        compiler_params=pltpu.CompilerParams(vmem_limit_bytes=40 << 20),
        cost_estimate=pl.CostEstimate(
            flops=2 * rows * depth * width, bytes_accessed=2 * depth * width, transcendentals=0
        ),
    )(features, *operands, *extra)


def on_device(query_in, key_in, value_in, residual, out_weight, gate_scale):
    own_rows = query_in.shape[0]
    rows = 8 * own_rows
    position = lax.axis_index("y") * 4 + lax.axis_index("x")
    height = out_weight.shape[0]
    sent = lax.dynamic_slice_in_dim(out_weight, position * (height // 16), height // 16, axis=0)
    crossed = flip(sent, "zh", "zl")
    other_weight = flip(out_weight, "c")

    stages = cut(query_in, key_in, value_in, (((2, 3),), ((0, 1), (4, 4))))
    got = exchange(stages[0], CZ).transpose(1, 0, 2, 3).reshape(3, 2, 4 * own_rows, LANES)
    got_second = exchange(stages[1], CZ)

    q, kv = got[0], got[1:].reshape(2, rows, LANES)
    kv_near, q_near = neighbours(kv, "y"), neighbours(q, "x")
    *parts, crossed = halves(kv_near, q_near, crossed, hand_on=True)
    far_weight = lax.all_gather(crossed, ("c", "y", "x"), tiled=True).reshape(2, height, -1)
    kv_far, q_far = far(parts[:2], "y"), far(parts[2:], "x")
    stage = ([q] + q_near + q_far, [kv] + kv_near + kv_far, own_rows, "x", (0, rows), None)

    q, kv = second_stage(got_second, q_far)
    kv_near, q_near = neighbours(kv, "y"), neighbours(q, "x")
    out, token = flash(*stage, (1, 2, 3))
    parts = halves(kv_near, q_near, token)
    kv_far, q_far = far(parts[:2], "y"), far(parts[2:], "x")
    out, _ = flash(*stage, (0,), out)

    stage = ([q] + q_near + q_far, [kv] + kv_near + kv_far, own_rows, "x")
    every, owners = (0, 1, 2, 3), ("x", "c", "zh", "zl")
    out, token = flash(*stage, (rows, rows // 2), 1, every, out, 1)
    first = merge(exchange(out, owners), own_rows)
    out, _ = flash(*stage, (0, rows), 0, every, token=token)
    last = merge(exchange(out, owners), own_rows)

    weights = [out_weight, other_weight, far_weight, far_weight]
    early = project(early_body, first, ((256, 1), (128, 4)), weights, (), F32)
    extra = (early, residual, gate_scale.reshape(1, -1))
    return project(late_body, last, ((256, 0),), weights, extra, BF16)


def solution(mesh):
    fine = Mesh(mesh.devices.reshape(tuple(SIZES.values())), ALL)
    tokens = P(ALL, None)
    return jax.shard_map(
        on_device,
        mesh=fine,
        in_specs=(tokens, tokens, tokens, tokens, P(("zh", "c"), None), P()),
        out_specs=tokens,
        check_vma=False,
    )
```

```python
import functools

import jax
import jax.numpy as jnp
from jax import lax
from jax.experimental import pallas as pl
from jax.experimental.pallas import tpu as pltpu
from jax.sharding import Mesh
from jax.sharding import PartitionSpec as P

HEAD_DIM = 128
LANES = 128
SCALE = HEAD_DIM**-0.5 * 1.4426950408889634
ALL = ("zh", "c", "y", "zl", "x")
SIZES = {"zh": 2, "c": 2, "y": 4, "zl": 2, "x": 4}
CZ = ("c", "zh", "zl")
KEY_TILE = 256
VMEM_BYTES = 20 << 20
F32 = jnp.float32
BF16 = jnp.bfloat16
NT = (((1,), (1,)), ((), ()))


def flip(x, *names):
    total = 2 ** len(names)
    return lax.ppermute(x, names, [(i, total - 1 - i) for i in range(total)])


def exchange(x, axes):
    return lax.all_to_all(x, axes, split_axis=0, concat_axis=0, tiled=True)


def shift(x, axis, by):
    n = SIZES[axis]
    return lax.ppermute(x, axis, [(i, (i + by) % n) for i in range(n)])


def neighbours(x, axis):
    return [shift(x, axis, 1), shift(x, axis, -1)]


def far(halves, axis):
    return [shift(halves[0], axis, 1), shift(halves[1], axis, -1)]


def halves_body(kv_left, kv_right, q_left, q_right, awaited, *outs):
    outs[0][...], outs[1][...] = kv_left[0], kv_right[1]
    outs[2][...], outs[3][...] = q_left[0], q_right[1]


def halves(kv_near, q_near, awaited):
    like = [kv_near[0][0], kv_near[1][1], q_near[0][0], q_near[1][1]]
    return pl.pallas_call(
        halves_body,
        out_shape=[jax.ShapeDtypeStruct(x.shape, x.dtype) for x in like],
        compiler_params=pltpu.CompilerParams(vmem_limit_bytes=VMEM_BYTES),
    )(*kv_near, *q_near, awaited)


def second_body(got, first_far, second_far, q, kv):
    core = lax.axis_index("c")
    for i in range(8):
        q[0, i], q[1, i] = got[i, 0], got[i, 3]
        kv[0, i], kv[1, i] = got[i, 1], got[i, 2]
    for z in range(4):
        kv[0, 8 + z], kv[1, 8 + z] = got[4 * core + z, 4], got[4 * core + z, 5]


def second_stage(got, earlier):
    rows = got.shape[2]
    shapes = [(2, 8, rows, LANES), (2, 12, rows, LANES)]
    q, kv = pl.pallas_call(
        second_body,
        out_shape=[jax.ShapeDtypeStruct(x, BF16) for x in shapes],
        compiler_params=pltpu.CompilerParams(vmem_limit_bytes=VMEM_BYTES),
    )(got, *earlier)
    return q.reshape(2, 8 * rows, LANES), kv.reshape(2, 12 * rows, LANES)


def cut_body(heads_of, q, k, v, *outs):
    for out, parts in zip(outs, heads_of):
        for part, heads in enumerate(parts):
            for c in range(2):
                for z in range(4):
                    first = (5 * z + heads[c]) * LANES
                    for i, x in enumerate((q, k, v)):
                        out[4 * c + z, 3 * part + i] = x[:, first : first + LANES]


def cut(q, k, v, heads_of):
    return pl.pallas_call(
        functools.partial(cut_body, heads_of),
        out_shape=[
            jax.ShapeDtypeStruct((8, 3 * len(parts), q.shape[0], LANES), BF16)
            for parts in heads_of
        ],
    )(q, k, v)


def eye(rows):
    return lax.broadcasted_iota(jnp.int32, (rows, LANES), 0) == lax.broadcasted_iota(
        jnp.int32, (rows, LANES), 1
    )


def write_block(out, at, part, result, level):
    rows = result.shape[0]
    line = jnp.sum(jnp.where(eye(rows), level, 0.0), axis=0, keepdims=True)
    high = line.astype(BF16).astype(F32)
    middle = (line - high).astype(BF16).astype(F32)
    spare = jnp.zeros((out.shape[2] - rows - 3, LANES), F32)
    block = [result, high, middle, line - high - middle, spare]
    out[at, part] = jnp.concatenate(block, axis=0).astype(BF16)


def read_level(block, rows):
    parts = block[-16:, :].astype(F32)
    at = rows - block.shape[0] + 16
    return parts[at : at + 1] + parts[at + 1 : at + 2] + parts[at + 2 : at + 3]


def attend(q, keys, values, n_keys):
    largest = total = None
    for start in range(0, n_keys, KEY_TILE):
        tile = pl.ds(start, min(KEY_TILE, n_keys - start))
        scores = lax.dot_general(q, keys[tile, :], NT, preferred_element_type=F32)
        new = jnp.max(scores, axis=1, keepdims=True)
        if total is not None:
            new = jnp.maximum(largest, new)
        weights = jnp.exp2((scores - new) * SCALE).astype(BF16)
        update = jnp.dot(weights, values[tile, :], preferred_element_type=F32)
        if total is None:
            total = update
        else:
            total = total * jnp.exp2((largest - new) * SCALE) + update
        largest = new
    sums = total[:, HEAD_DIM:]
    return total[:, :HEAD_DIM] / sums, largest * SCALE + jnp.log2(sums)


def lay_out(kv_own, kv_left, kv_right, k_far, v_far, first_key, key_rows, keys, values):
    these = slice(first_key, first_key + key_rows)
    for i, ref in enumerate((kv_own, kv_left, kv_right)):
        to = slice(i * key_rows, (i + 1) * key_rows)
        keys[to, :] = ref[0, these, :]
        values[to, :HEAD_DIM] = ref[1, these, :]
    to = slice(3 * key_rows, 4 * key_rows)
    keys[to, :] = k_far[these, :]
    values[to, :HEAD_DIM] = v_far[these, :]


def first_body(rows, units, based, *refs):
    q_own, q_left, q_right, *q_far = refs[:5]
    base = refs[10]
    out, token, keys, values = refs[-4:]
    token[...] = jnp.zeros_like(token)
    values[:, HEAD_DIM:] = jnp.ones((values.shape[0], LANES), BF16)
    lay_out(*refs[5:10], 0, 8 * rows, keys, values)
    me, zh = lax.axis_index("x"), lax.axis_index("zh")
    if based:
        for unit in range(4):
            if unit not in units:
                for k in range(8):
                    at = 8 * lax.rem(me + unit, 4) + k
                    out[at, 0] = base[at, 0]
    for unit in units:
        if unit == 2:
            q = jnp.concatenate([q_far[0][...], q_far[1][...]], axis=0)
        else:
            q = {0: q_own, 1: q_right, 3: q_left}[unit][...].reshape(8 * rows, HEAD_DIM)
        result, level = attend(q, keys, values, 32 * rows)
        for k in range(8):
            c, z = divmod(k, 4)
            own = zh if z // 2 else 1 - zh
            z_lo = own * (z % 2) + (1 - own) * (1 - z % 2)
            here = slice(k * rows, (k + 1) * rows)
            at = 8 * lax.rem(me + unit, 4) + 4 * c + 2 * z_lo + own
            write_block(out, at, 0, result[here], level[here])


def second_half_body(rows, own, *refs):
    q_own, q_left, q_right, *q_far = refs[:5]
    out, token, keys, values = refs[-4:]
    token[...] = jnp.zeros_like(token)
    values[:, HEAD_DIM:] = jnp.ones((values.shape[0], LANES), BF16)
    me, zh = lax.axis_index("x"), lax.axis_index("zh")
    side = zh if own else 1 - zh
    for part, (first_key, key_rows) in enumerate(((0, 8 * rows), (8 * rows, 4 * rows))):
        lay_out(*refs[5:10], first_key, key_rows, keys, values)

        def query(unit, c):
            here = pl.ds(pl.multiple_of(4 * c * rows + 2 * side * rows, 2 * rows), 2 * rows)
            if unit == 2:
                return q_far[part][here, :]
            return {0: q_own, 1: q_right, 3: q_left}[unit][part, here, :]

        for units in ((0, 1), (2, 3)):
            q = jnp.concatenate([query(unit, c) for unit in units for c in range(2)], axis=0)
            result, level = attend(q, keys, values, 4 * key_rows)
            k = 0
            for unit in units:
                for c in range(2):
                    for i in range(2):
                        here = slice(k * rows, (k + 1) * rows)
                        at = 4 * lax.rem(me + unit, 4) + 2 * c + (i if own else 1 - i)
                        write_block(out, at, part, result[here], level[here])
                        k += 1


def flash(body, blocks, parts, rows, share, operands):
    pairs = int(share * 32 * rows * 32 * rows * (1.5 if parts > 1 else 1))
    return pl.pallas_call(
        body,
        out_shape=[
            jax.ShapeDtypeStruct((blocks, parts, -(-(rows + 3) // 16) * 16, LANES), BF16),
            jax.ShapeDtypeStruct((8, LANES), F32),
        ],
        scratch_shapes=[
            pltpu.VMEM((32 * rows, HEAD_DIM), BF16),
            pltpu.VMEM((32 * rows, 2 * HEAD_DIM), BF16),
        ],
        compiler_params=pltpu.CompilerParams(vmem_limit_bytes=VMEM_BYTES),
        cost_estimate=pl.CostEstimate(
            flops=8 * pairs * HEAD_DIM, bytes_accessed=4 << 20, transcendentals=pairs
        ),
    )(*operands)


def merge_blocks(blocks, rows):
    levels = [read_level(b, rows) for b in blocks]
    top = functools.reduce(jnp.maximum, levels)
    shares = [jnp.exp2(v - top) for v in levels]
    whole = functools.reduce(jnp.add, shares)
    total = 0.0
    for share, b in zip(shares, blocks):
        wide = jnp.broadcast_to((share / whole)[:, :rows], (rows, rows))
        diagonal = jnp.where(eye(rows)[:, :rows], wide, 0.0).astype(BF16)
        total = total + jnp.dot(diagonal, b[:rows, :], preferred_element_type=F32)
    return total.astype(BF16)


def merge_first_body(x, token, out):
    rows = out.shape[2]
    for own in range(2):
        for z in range(2):
            for c in range(2):
                blocks = [x[8 * i + 4 * c + 2 * z + own, 0] for i in range(4)]
                out[own, z, :, c * LANES : (c + 1) * LANES] = merge_blocks(blocks, rows)


def merge_second_body(x, token, out):
    rows = out.shape[1]
    for z in range(2):
        for c in range(2):
            value = merge_blocks([x[4 * i + 2 * c + z, 0] for i in range(4)], rows)
            out[z, :, c * LANES : (c + 1) * LANES] = value
        both = [x[4 * i + 2 * c + z, 1] for i in range(4) for c in range(2)]
        out[z, :, 2 * LANES :] = merge_blocks(both, rows)


def merge(body, x, token, shape):
    return pl.pallas_call(
        body,
        out_shape=jax.ShapeDtypeStruct(shape, BF16),
        compiler_params=pltpu.CompilerParams(vmem_limit_bytes=VMEM_BYTES),
    )(x, token)


def on_device(query_in, key_in, value_in, residual, out_weight, gate_scale):
    own_rows = query_in.shape[0]
    rows = 8 * own_rows
    core = lax.axis_index("c")
    other_weight = flip(out_weight, "c")

    stages = cut(query_in, key_in, value_in, (((0, 1),), ((2, 3), (4, 4))))
    got = exchange(stages[0], CZ).transpose(1, 0, 2, 3).reshape(3, 2, 4 * own_rows, LANES)
    got_second = exchange(stages[1], CZ)

    q, kv = got[0], got[1:].reshape(2, rows, LANES)
    kv_near, q_near = neighbours(kv, "y"), neighbours(q, "x")
    parts = halves(kv_near, q_near, got_second)
    kv_far, q_far = far(parts[:2], "y"), far(parts[2:], "x")
    stage = [q] + q_near + q_far + [kv] + kv_near + kv_far

    q, kv = second_stage(got_second, q_far)
    kv_near, q_near = neighbours(kv, "y"), neighbours(q, "x")
    body = functools.partial(first_body, own_rows, (1, 2, 3), False)
    out, token = flash(body, 32, 1, own_rows, 0.75, stage)
    parts = halves(kv_near, q_near, token)
    kv_far, q_far = far(parts[:2], "y"), far(parts[2:], "x")
    body = functools.partial(first_body, own_rows, (0,), True)
    out, token = flash(body, 32, 1, own_rows, 0.25, stage + [out, parts[2]])

    owners = ("x", "c", "zl")
    first = exchange(out, owners)
    stage = [q] + q_near + q_far + [kv] + kv_near + kv_far

    crossing, token = flash(
        functools.partial(second_half_body, own_rows, False), 16, 2, own_rows, 0.5, stage + [token]
    )
    first = merge(merge_first_body, first, token, (2, 2, own_rows, 2 * LANES))
    crossing = exchange(crossing, owners)
    own, token = flash(
        functools.partial(second_half_body, own_rows, True), 16, 2, own_rows, 0.5, stage + [token]
    )
    shape = (2, own_rows, 3 * LANES)
    crossing = merge(merge_second_body, crossing, token, shape)
    own = merge(merge_second_body, exchange(own, owners), token, shape)

    def product(features):
        for_own = jnp.where(core == 0, features[0], features[1])
        for_other = jnp.where(core == 0, features[1], features[0])
        return jnp.dot(for_own, out_weight, preferred_element_type=F32) + jnp.dot(
            for_other, other_weight, preferred_element_type=F32
        )

    theirs = product(jnp.concatenate([first[0], crossing], axis=2)).astype(BF16)
    ours = product(jnp.concatenate([first[1], own], axis=2))
    projected = ours + flip(theirs, "zh", "zl").astype(F32)
    return (residual.astype(F32) + gate_scale * projected).astype(BF16)


def solution(mesh):
    fine = Mesh(mesh.devices.reshape(tuple(SIZES.values())), ALL)
    tokens = P(ALL, None)
    return jax.shard_map(
        on_device,
        mesh=fine,
        in_specs=(tokens, tokens, tokens, tokens, P(("zh", "c"), None), P()),
        out_specs=tokens,
        check_vma=False,
    )
```

```python
import functools

import jax
import jax.numpy as jnp
from jax import lax
from jax.experimental import pallas as pl
from jax.experimental.pallas import tpu as pltpu
from jax.sharding import Mesh
from jax.sharding import PartitionSpec as P

HEAD_DIM = 128
LANES = 128
SCALE = HEAD_DIM**-0.5 * 1.4426950408889634
ALL = ("zh", "c", "y", "zl", "x")
SIZES = {"zh": 2, "c": 2, "y": 4, "zl": 2, "x": 4}
CZ = ("c", "zh", "zl")
KEY_TILE = 256
VMEM_BYTES = 20 << 20
F32 = jnp.float32
BF16 = jnp.bfloat16
NT = (((1,), (1,)), ((), ()))


def flip(x, *names):
    total = 2 ** len(names)
    return lax.ppermute(x, names, [(i, total - 1 - i) for i in range(total)])


def exchange(x, axes):
    return lax.all_to_all(x, axes, split_axis=0, concat_axis=0, tiled=True)


def shift(x, axis, by):
    n = SIZES[axis]
    return lax.ppermute(x, axis, [(i, (i + by) % n) for i in range(n)])


def neighbours(x, axis):
    return [shift(x, axis, 1), shift(x, axis, -1)]


def far(halves, axis):
    return [shift(halves[0], axis, 1), shift(halves[1], axis, -1)]


def halves_body(kv_left, kv_right, q_left, q_right, awaited, *outs):
    outs[0][...], outs[1][...] = kv_left[0], kv_right[1]
    outs[2][...], outs[3][...] = q_left[0], q_right[1]


def halves(kv_near, q_near, awaited):
    like = [kv_near[0][0], kv_near[1][1], q_near[0][0], q_near[1][1]]
    return pl.pallas_call(
        halves_body,
        out_shape=[jax.ShapeDtypeStruct(x.shape, x.dtype) for x in like],
        compiler_params=pltpu.CompilerParams(vmem_limit_bytes=VMEM_BYTES),
    )(*kv_near, *q_near, awaited)


def second_body(got, first_far, second_far, q, kv):
    core = lax.axis_index("c")
    for i in range(8):
        q[0, i], q[1, i] = got[i, 0], got[i, 3]
        kv[0, i], kv[1, i] = got[i, 1], got[i, 2]
    for z in range(4):
        kv[0, 8 + z], kv[1, 8 + z] = got[4 * core + z, 4], got[4 * core + z, 5]


def second_stage(got, earlier):
    rows = got.shape[2]
    shapes = [(2, 8, rows, LANES), (2, 12, rows, LANES)]
    q, kv = pl.pallas_call(
        second_body,
        out_shape=[jax.ShapeDtypeStruct(x, BF16) for x in shapes],
        compiler_params=pltpu.CompilerParams(vmem_limit_bytes=VMEM_BYTES),
    )(got, *earlier)
    return q.reshape(2, 8 * rows, LANES), kv.reshape(2, 12 * rows, LANES)


def cut_body(heads_of, q, k, v, *outs):
    for out, parts in zip(outs, heads_of):
        for part, heads in enumerate(parts):
            for c in range(2):
                for z in range(4):
                    first = (5 * z + heads[c]) * LANES
                    for i, x in enumerate((q, k, v)):
                        out[4 * c + z, 3 * part + i] = x[:, first : first + LANES]


def cut(q, k, v, heads_of):
    return pl.pallas_call(
        functools.partial(cut_body, heads_of),
        out_shape=[
            jax.ShapeDtypeStruct((8, 3 * len(parts), q.shape[0], LANES), BF16)
            for parts in heads_of
        ],
    )(q, k, v)


def eye(rows):
    return lax.broadcasted_iota(jnp.int32, (rows, LANES), 0) == lax.broadcasted_iota(
        jnp.int32, (rows, LANES), 1
    )


def write_block(out, at, part, result, level):
    rows = result.shape[0]
    line = jnp.sum(jnp.where(eye(rows), level, 0.0), axis=0, keepdims=True)
    high = line.astype(BF16).astype(F32)
    middle = (line - high).astype(BF16).astype(F32)
    spare = jnp.zeros((out.shape[2] - rows - 3, LANES), F32)
    block = [result, high, middle, line - high - middle, spare]
    out[at, part] = jnp.concatenate(block, axis=0).astype(BF16)


def read_level(block, rows):
    parts = block[-16:, :].astype(F32)
    at = rows - block.shape[0] + 16
    return parts[at : at + 1] + parts[at + 1 : at + 2] + parts[at + 2 : at + 3]


def attend(q, keys, values, first, n_keys):
    largest = total = None
    for start in range(first, first + n_keys, KEY_TILE):
        tile = pl.ds(start, min(KEY_TILE, first + n_keys - start))
        scores = lax.dot_general(q, keys[tile, :], NT, preferred_element_type=F32)
        new = jnp.max(scores, axis=1, keepdims=True)
        if total is not None:
            new = jnp.maximum(largest, new)
        weights = jnp.exp2((scores - new) * SCALE).astype(BF16)
        update = jnp.dot(weights, values[tile, :], preferred_element_type=F32)
        if total is None:
            total = update
        else:
            total = total * jnp.exp2((largest - new) * SCALE) + update
        largest = new
    sums = total[:, HEAD_DIM:]
    return total[:, :HEAD_DIM] / sums, largest * SCALE + jnp.log2(sums)


def place_keys(kv, first_key, key_rows, keys, values, at):
    kv_own, kv_left, kv_right, k_far, v_far = kv
    these = pl.ds(first_key, key_rows)
    copies = []
    for i, ref in enumerate((kv_own, kv_left, kv_right, None)):
        to = pl.ds(at + i * key_rows, key_rows)
        k = k_far.at[these, :] if ref is None else ref.at[0, these, :]
        v = v_far.at[these, :] if ref is None else ref.at[1, these, :]
        copies += [(k, keys.at[to, :]), (v, values.at[to, pl.ds(0, HEAD_DIM)])]
    return copies


def run(copies, sems):
    started = []
    for i, (source, target) in enumerate(copies):
        copy = pltpu.make_async_copy(source, target, sems.at[i])
        copy.start()
        started.append(copy)
    return started


def first_body(rows, units, based, *refs):
    q_own, q_left, q_right, q_far_a, q_far_b = refs[:5]
    base = refs[10]
    out, token, keys, values, queries, sems = refs[-6:]
    me, zh = lax.axis_index("x"), lax.axis_index("zh")
    copies = place_keys(refs[5:10], 0, 8 * rows, keys, values, 0)
    for unit in units:
        if unit == 2:
            copies += [(q_far_a, queries.at[2, 0]), (q_far_b, queries.at[2, 1])]
        else:
            copies.append(({0: q_own, 1: q_right, 3: q_left}[unit], queries.at[unit]))
    if based:
        for unit in range(4):
            if unit not in units:
                here = pl.ds(8 * lax.rem(me + unit, 4), 8)
                copies.append((base.at[here], out.at[here]))
    started = run(copies, sems)
    token[...] = jnp.zeros_like(token)
    values[:, HEAD_DIM:] = jnp.ones((values.shape[0], LANES), BF16)
    for copy in started:
        copy.wait()
    for unit in units:
        q = queries[unit].reshape(8 * rows, HEAD_DIM)
        result, level = attend(q, keys, values, 0, 32 * rows)
        for k in range(8):
            c, z = divmod(k, 4)
            own = zh if z // 2 else 1 - zh
            z_lo = own * (z % 2) + (1 - own) * (1 - z % 2)
            here = slice(k * rows, (k + 1) * rows)
            at = 8 * lax.rem(me + unit, 4) + 4 * c + 2 * z_lo + own
            write_block(out, at, 0, result[here], level[here])


def second_half_body(rows, own, *refs):
    q_own, q_left, q_right, q_far_a, q_far_b = refs[:5]
    out, token, keys, values, queries, sems = refs[-6:]
    me, zh = lax.axis_index("x"), lax.axis_index("zh")
    side = zh if own else 1 - zh
    heads = ((0, 8 * rows, 0), (8 * rows, 4 * rows, 32 * rows))
    copies = [(q_own, queries.at[0]), (q_right, queries.at[1]), (q_left, queries.at[3])]
    copies += [(q_far_a, queries.at[2, 0]), (q_far_b, queries.at[2, 1])]
    for first_key, key_rows, at in heads:
        copies += place_keys(refs[5:10], first_key, key_rows, keys, values, at)
    started = run(copies, sems)
    token[...] = jnp.zeros_like(token)
    values[:, HEAD_DIM:] = jnp.ones((values.shape[0], LANES), BF16)
    for copy in started[:13]:
        copy.wait()
    for part, (first_key, key_rows, first) in enumerate(heads):
        if part == 1:
            for copy in started[13:]:
                copy.wait()

        def query(unit, c):
            here = pl.ds(pl.multiple_of(4 * c * rows + 2 * side * rows, 2 * rows), 2 * rows)
            return queries[unit, part, here, :]

        for units in ((0, 1), (2, 3)):
            q = jnp.concatenate([query(unit, c) for unit in units for c in range(2)], axis=0)
            result, level = attend(q, keys, values, first, 4 * key_rows)
            k = 0
            for unit in units:
                for c in range(2):
                    for i in range(2):
                        here = slice(k * rows, (k + 1) * rows)
                        at = 4 * lax.rem(me + unit, 4) + 2 * c + (i if own else 1 - i)
                        write_block(out, at, part, result[here], level[here])
                        k += 1


def flash(body, blocks, parts, rows, share, operands):
    pairs = int(share * 32 * rows * 32 * rows * (1.5 if parts > 1 else 1))
    return pl.pallas_call(
        body,
        out_shape=[
            jax.ShapeDtypeStruct((blocks, parts, -(-(rows + 3) // 16) * 16, LANES), BF16),
            jax.ShapeDtypeStruct((8, LANES), F32),
        ],
        in_specs=[pl.BlockSpec(memory_space=pltpu.HBM)] * len(operands),
        scratch_shapes=[
            pltpu.VMEM((16 * (parts + 1) * rows, HEAD_DIM), BF16),
            pltpu.VMEM((16 * (parts + 1) * rows, 2 * HEAD_DIM), BF16),
            pltpu.VMEM((4, 2, (8 if parts > 1 else 4) * rows, HEAD_DIM), BF16),
            pltpu.SemaphoreType.DMA((24,)),
        ],
        compiler_params=pltpu.CompilerParams(vmem_limit_bytes=60 << 20),
        cost_estimate=pl.CostEstimate(
            flops=8 * pairs * HEAD_DIM, bytes_accessed=4 << 20, transcendentals=pairs
        ),
    )(*operands)


def merge_blocks(blocks, rows):
    levels = [read_level(b, rows) for b in blocks]
    top = functools.reduce(jnp.maximum, levels)
    shares = [jnp.exp2(v - top) for v in levels]
    whole = functools.reduce(jnp.add, shares)
    total = 0.0
    for share, b in zip(shares, blocks):
        wide = jnp.broadcast_to((share / whole)[:, :rows], (rows, rows))
        diagonal = jnp.where(eye(rows)[:, :rows], wide, 0.0).astype(BF16)
        total = total + jnp.dot(diagonal, b[:rows, :], preferred_element_type=F32)
    return total.astype(BF16)


def merge_first_body(x, token, out):
    rows = out.shape[2]
    for own in range(2):
        for z in range(2):
            for c in range(2):
                blocks = [x[8 * i + 4 * c + 2 * z + own, 0] for i in range(4)]
                out[own, z, :, c * LANES : (c + 1) * LANES] = merge_blocks(blocks, rows)


def merge_second_body(x, token, out):
    rows = out.shape[1]
    for z in range(2):
        for c in range(2):
            value = merge_blocks([x[4 * i + 2 * c + z, 0] for i in range(4)], rows)
            out[z, :, c * LANES : (c + 1) * LANES] = value
        both = [x[4 * i + 2 * c + z, 1] for i in range(4) for c in range(2)]
        out[z, :, 2 * LANES :] = merge_blocks(both, rows)


def merge(body, x, token, shape):
    return pl.pallas_call(
        body,
        out_shape=jax.ShapeDtypeStruct(shape, BF16),
        compiler_params=pltpu.CompilerParams(vmem_limit_bytes=VMEM_BYTES),
    )(x, token)


def on_device(query_in, key_in, value_in, residual, out_weight, gate_scale):
    own_rows = query_in.shape[0]
    rows = 8 * own_rows
    core = lax.axis_index("c")
    other_weight = flip(out_weight, "c")

    stages = cut(query_in, key_in, value_in, (((0, 1),), ((2, 3), (4, 4))))
    got = exchange(stages[0], CZ).transpose(1, 0, 2, 3).reshape(3, 2, 4 * own_rows, LANES)
    got_second = exchange(stages[1], CZ)

    q, kv = got[0], got[1:].reshape(2, rows, LANES)
    kv_near, q_near = neighbours(kv, "y"), neighbours(q, "x")
    parts = halves(kv_near, q_near, got_second)
    kv_far, q_far = far(parts[:2], "y"), far(parts[2:], "x")
    stage = [q] + q_near + q_far + [kv] + kv_near + kv_far

    q, kv = second_stage(got_second, q_far)
    kv_near, q_near = neighbours(kv, "y"), neighbours(q, "x")
    body = functools.partial(first_body, own_rows, (1, 2, 3), False)
    out, token = flash(body, 32, 1, own_rows, 0.75, stage)
    parts = halves(kv_near, q_near, token)
    kv_far, q_far = far(parts[:2], "y"), far(parts[2:], "x")
    body = functools.partial(first_body, own_rows, (0,), True)
    out, token = flash(body, 32, 1, own_rows, 0.25, stage + [out, parts[2]])

    owners = ("x", "c", "zl")
    first = exchange(out, owners)
    stage = [q] + q_near + q_far + [kv] + kv_near + kv_far

    crossing, token = flash(
        functools.partial(second_half_body, own_rows, False), 16, 2, own_rows, 0.5, stage + [token]
    )
    first = merge(merge_first_body, first, token, (2, 2, own_rows, 2 * LANES))
    crossing = exchange(crossing, owners)
    own, token = flash(
        functools.partial(second_half_body, own_rows, True), 16, 2, own_rows, 0.5, stage + [token]
    )
    shape = (2, own_rows, 3 * LANES)
    crossing = merge(merge_second_body, crossing, token, shape)
    own = merge(merge_second_body, exchange(own, owners), token, shape)

    def product(features):
        for_own = jnp.where(core == 0, features[0], features[1])
        for_other = jnp.where(core == 0, features[1], features[0])
        return jnp.dot(for_own, out_weight, preferred_element_type=F32) + jnp.dot(
            for_other, other_weight, preferred_element_type=F32
        )

    theirs = product(jnp.concatenate([first[0], crossing], axis=2)).astype(BF16)
    ours = lax.optimization_barrier(product(jnp.concatenate([first[1], own], axis=2)))
    projected = ours + flip(theirs, "zh", "zl").astype(F32)
    return (residual.astype(F32) + gate_scale * projected).astype(BF16)


def solution(mesh):
    fine = Mesh(mesh.devices.reshape(tuple(SIZES.values())), ALL)
    tokens = P(ALL, None)
    return jax.shard_map(
        on_device,
        mesh=fine,
        in_specs=(tokens, tokens, tokens, tokens, P(("zh", "c"), None), P()),
        out_specs=tokens,
        check_vma=False,
    )
```

```python
import functools

import jax
import jax.numpy as jnp
from jax import lax
from jax.experimental import pallas as pl
from jax.experimental.pallas import tpu as pltpu
from jax.sharding import Mesh
from jax.sharding import PartitionSpec as P

HEAD_DIM = 128
LANES = 128
SCALE = HEAD_DIM**-0.5 * 1.4426950408889634
ALL = ("zh", "c", "y", "zl", "x")
SIZES = {"zh": 2, "c": 2, "y": 4, "zl": 2, "x": 4}
CZ = ("c", "zh", "zl")
KEY_TILE = 256
VMEM_BYTES = 20 << 20
F32 = jnp.float32
BF16 = jnp.bfloat16
NT = (((1,), (1,)), ((), ()))


def flip(x, *names):
    total = 2 ** len(names)
    return lax.ppermute(x, names, [(i, total - 1 - i) for i in range(total)])


def exchange(x, axes):
    return lax.all_to_all(x, axes, split_axis=0, concat_axis=0, tiled=True)


def shift(x, axis, by):
    n = SIZES[axis]
    return lax.ppermute(x, axis, [(i, (i + by) % n) for i in range(n)])


def neighbours(x, axis):
    return [shift(x, axis, 1), shift(x, axis, -1)]


def far(halves, axis):
    return [shift(halves[0], axis, 1), shift(halves[1], axis, -1)]


def halves_body(kv_left, kv_right, q_left, q_right, awaited, *outs):
    outs[0][...], outs[1][...] = kv_left[0], kv_right[1]
    outs[2][...], outs[3][...] = q_left[0], q_right[1]


def halves(kv_near, q_near, awaited):
    like = [kv_near[0][0], kv_near[1][1], q_near[0][0], q_near[1][1]]
    return pl.pallas_call(
        halves_body,
        out_shape=[jax.ShapeDtypeStruct(x.shape, x.dtype) for x in like],
        compiler_params=pltpu.CompilerParams(vmem_limit_bytes=VMEM_BYTES),
    )(*kv_near, *q_near, awaited)


def cut_body(heads_of, q, k, v, out):
    for part, heads in enumerate(heads_of):
        for c in range(2):
            for z in range(4):
                first = (5 * z + heads[c]) * LANES
                for i, x in enumerate((q, k, v)):
                    out[4 * c + z, 3 * part + i] = x[:, first : first + LANES]


def cut(q, k, v, heads_of):
    return pl.pallas_call(
        functools.partial(cut_body, heads_of),
        out_shape=jax.ShapeDtypeStruct((8, 3 * len(heads_of), q.shape[0], LANES), BF16),
    )(q, k, v)


def arrange_body(got, q, kv):
    core = lax.axis_index("c")
    for c in range(2):
        for z in range(4):
            for part in range(3):
                q[c, 4 * part + z] = got[4 * c + z, 3 * part]
            for part in range(2):
                for i in range(2):
                    kv[i, 8 * part + 4 * c + z] = got[4 * c + z, 3 * part + 1 + i]
    for z in range(4):
        for i in range(2):
            kv[i, 16 + z] = got[4 * core + z, 7 + i]


def arrange(got):
    rows = got.shape[2]
    shapes = [(2, 12, rows, LANES), (2, 20, rows, LANES)]
    q, kv = pl.pallas_call(
        arrange_body,
        out_shape=[jax.ShapeDtypeStruct(x, BF16) for x in shapes],
        compiler_params=pltpu.CompilerParams(vmem_limit_bytes=VMEM_BYTES),
    )(got)
    return q.reshape(2, 12 * rows, LANES), kv.reshape(2, 20 * rows, LANES)


def eye(rows):
    return lax.broadcasted_iota(jnp.int32, (rows, LANES), 0) == lax.broadcasted_iota(
        jnp.int32, (rows, LANES), 1
    )


def write_block(out, at, part, result, level):
    rows = result.shape[0]
    line = jnp.sum(jnp.where(eye(rows), level, 0.0), axis=0, keepdims=True)
    high = line.astype(BF16).astype(F32)
    middle = (line - high).astype(BF16).astype(F32)
    spare = jnp.zeros((out.shape[2] - rows - 3, LANES), F32)
    block = [result, high, middle, line - high - middle, spare]
    out[at, part] = jnp.concatenate(block, axis=0).astype(BF16)


def read_level(block, rows):
    parts = block[-16:, :].astype(F32)
    at = rows - block.shape[0] + 16
    return parts[at : at + 1] + parts[at + 1 : at + 2] + parts[at + 2 : at + 3]


def attend(q, keys, values, first, n_keys, state=None):
    largest, total = state or (None, None)
    for start in range(first, first + n_keys, KEY_TILE):
        tile = pl.ds(start, min(KEY_TILE, first + n_keys - start))
        scores = lax.dot_general(q, keys[tile, :], NT, preferred_element_type=F32)
        new = jnp.max(scores, axis=1, keepdims=True)
        if total is not None:
            new = jnp.maximum(largest, new)
        weights = jnp.exp2((scores - new) * SCALE).astype(BF16)
        update = jnp.dot(weights, values[tile, :], preferred_element_type=F32)
        if total is None:
            total = update
        else:
            total = total * jnp.exp2((largest - new) * SCALE) + update
        largest = new
    return largest, total


def heads_at(rows):
    return ((0, 8 * rows), (8 * rows, 8 * rows), (16 * rows, 4 * rows))


def place_keys(kv, first_key, key_rows, keys, values, at):
    these = pl.ds(first_key, key_rows)
    copies = []
    for i, ref in enumerate(kv):
        to = pl.ds(at + i * key_rows, key_rows)
        if isinstance(ref, tuple):
            k, v = ref[0].at[these, :], ref[1].at[these, :]
        else:
            k, v = ref.at[0, these, :], ref.at[1, these, :]
        copies += [(k, keys.at[to, :]), (v, values.at[to, pl.ds(0, HEAD_DIM)])]
    return copies


def run(copies, sems, at):
    started = []
    for i, (source, target) in enumerate(copies):
        copy = pltpu.make_async_copy(source, target, sems.at[at + i])
        copy.start()
        started.append(copy)
    return started


def start_all(copies, kv, rows, keys, values, sems):
    groups, at, row = [], 0, 0
    for part, (first_key, key_rows) in enumerate(heads_at(rows)):
        here = place_keys(kv, first_key, key_rows, keys, values, row)
        if part == 0:
            here = copies + here
        groups.append(run(here, sems, at))
        at += len(here)
        row += len(kv) * key_rows
    values[:, HEAD_DIM:] = jnp.ones((values.shape[0], LANES), BF16)
    return groups


def half_queries(queries, unit, part, side, rows):
    pieces = []
    for c in range(2):
        at = 4 * part * rows + 2 * side * rows
        pieces.append(queries[unit, c, pl.ds(pl.multiple_of(at, 2 * rows), 2 * rows), :])
    return pieces


def write_unit(out, unit, part, own, rows, largest, total):
    me = lax.axis_index("x")
    result = total[:, :HEAD_DIM] / total[:, HEAD_DIM:]
    level = largest * SCALE + jnp.log2(total[:, HEAD_DIM:])
    for c in range(2):
        for i in range(2):
            k = 2 * c + i
            here = slice(k * rows, (k + 1) * rows)
            at = 4 * lax.rem(me + unit, 4) + 2 * c + (i if own else 1 - i)
            write_block(out, at, part, result[here], level[here])


NEAR = (0, 1, 3)


def near_body(rows, *refs):
    q_own, q_left, q_right, *kv = refs[:6]
    total_out, stat_out, keys, values, queries, sems = refs[-6:]
    side = 1 - lax.axis_index("zh")
    copies = [(q_own, queries.at[0]), (q_right, queries.at[1]), (q_left, queries.at[3])]
    groups = start_all(copies, kv, rows, keys, values, sems)
    row = 0
    for part, (_, key_rows) in enumerate(heads_at(rows)):
        for copy in groups[part]:
            copy.wait()
        q = sum((half_queries(queries, unit, part, side, rows) for unit in NEAR), [])
        largest, total = attend(jnp.concatenate(q, axis=0), keys, values, row, 3 * key_rows)
        total_out[part] = total[:, :HEAD_DIM]
        lane = lax.broadcasted_iota(jnp.int32, (12 * rows, LANES), 1)
        stat_out[part] = jnp.where(lane == 0, largest, total[:, HEAD_DIM:])
        row += 3 * key_rows


def rest_body(rows, *refs):
    q_far, kv, state = refs[3:5], refs[5:10], refs[10:12]
    out, token, keys, values, queries, total_in, stat_in, sems = refs[-8:]
    q_own, q_left, q_right = refs[:3]
    side = 1 - lax.axis_index("zh")
    copies = [(q_own, queries.at[0]), (q_right, queries.at[1]), (q_left, queries.at[3])]
    copies += [(q_far[0], queries.at[2, 0]), (q_far[1], queries.at[2, 1])]
    copies += [(state[0], total_in), (state[1], stat_in)]
    kv = [*kv[:3], (kv[3], kv[4])]
    groups = start_all(copies, kv, rows, keys, values, sems)
    token[...] = jnp.zeros_like(token)
    row = 0
    for part, (_, key_rows) in enumerate(heads_at(rows)):
        for copy in groups[part]:
            copy.wait()
        q = jnp.concatenate(half_queries(queries, 2, part, side, rows), axis=0)
        write_unit(out, 2, part, False, rows, *attend(q, keys, values, row, 4 * key_rows))
        q = sum((half_queries(queries, unit, part, side, rows) for unit in NEAR), [])
        stat = stat_in[part]
        lane = lax.broadcasted_iota(jnp.int32, stat.shape, 1)
        largest = jnp.max(jnp.where(lane == 0, stat, -jnp.inf), axis=1, keepdims=True)
        sums = jnp.sum(jnp.where(lane == 1, stat, 0.0), axis=1, keepdims=True)
        sums = jnp.broadcast_to(sums, stat.shape)
        before = (largest, jnp.concatenate([total_in[part], sums], axis=1))
        q = jnp.concatenate(q, axis=0)
        largest, total = attend(q, keys, values, row + 3 * key_rows, key_rows, before)
        for i, unit in enumerate(NEAR):
            here = slice(4 * i * rows, 4 * (i + 1) * rows)
            write_unit(out, unit, part, False, rows, largest[here], total[here])
        row += 4 * key_rows


def whole_body(rows, *refs):
    q_own, q_left, q_right, q_far_a, q_far_b = refs[:5]
    out, token, keys, values, queries, sems = refs[-6:]
    side = lax.axis_index("zh")
    copies = [(q_own, queries.at[0]), (q_right, queries.at[1]), (q_left, queries.at[3])]
    copies += [(q_far_a, queries.at[2, 0]), (q_far_b, queries.at[2, 1])]
    kv = [*refs[5:8], (refs[8], refs[9])]
    groups = start_all(copies, kv, rows, keys, values, sems)
    token[...] = jnp.zeros_like(token)
    row = 0
    for part, (_, key_rows) in enumerate(heads_at(rows)):
        for copy in groups[part]:
            copy.wait()
        for units in ((0, 1), (2, 3)):
            q = sum((half_queries(queries, unit, part, side, rows) for unit in units), [])
            largest, total = attend(jnp.concatenate(q, axis=0), keys, values, row, 4 * key_rows)
            for i, unit in enumerate(units):
                here = slice(4 * i * rows, 4 * (i + 1) * rows)
                write_unit(out, unit, part, True, rows, largest[here], total[here])
        row += 4 * key_rows


def flash(body, out_shape, rows, units, share, operands, scratch=()):
    pairs = int(share * 32 * rows * 80 * rows)
    key_rows = units * 20 * rows
    return pl.pallas_call(
        functools.partial(body, rows),
        out_shape=out_shape,
        in_specs=[pl.BlockSpec(memory_space=pltpu.HBM)] * len(operands),
        scratch_shapes=[
            pltpu.VMEM((key_rows, HEAD_DIM), BF16),
            pltpu.VMEM((key_rows, 2 * HEAD_DIM), BF16),
            pltpu.VMEM((4, 2, 12 * rows, HEAD_DIM), BF16),
            *scratch,
            pltpu.SemaphoreType.DMA((32,)),
        ],
        compiler_params=pltpu.CompilerParams(vmem_limit_bytes=60 << 20),
        cost_estimate=pl.CostEstimate(
            flops=8 * pairs * HEAD_DIM, bytes_accessed=8 << 20, transcendentals=pairs
        ),
    )(*operands)


def merge_blocks(blocks, rows):
    levels = [read_level(b, rows) for b in blocks]
    top = functools.reduce(jnp.maximum, levels)
    shares = [jnp.exp2(v - top) for v in levels]
    whole = functools.reduce(jnp.add, shares)
    total = 0.0
    for share, b in zip(shares, blocks):
        wide = jnp.broadcast_to((share / whole)[:, :rows], (rows, rows))
        diagonal = jnp.where(eye(rows)[:, :rows], wide, 0.0).astype(BF16)
        total = total + jnp.dot(diagonal, b[:rows, :], preferred_element_type=F32)
    return total.astype(BF16)


def merge_body(x, token, out):
    rows = out.shape[1]
    for z in range(2):
        for c in range(2):
            for part in range(2):
                value = merge_blocks([x[4 * i + 2 * c + z, part] for i in range(4)], rows)
                head = 2 * c + part
                out[z, :, head * LANES : (head + 1) * LANES] = value
        both = [x[4 * i + 2 * c + z, 2] for i in range(4) for c in range(2)]
        out[z, :, 4 * LANES :] = merge_blocks(both, rows)


def merge(x, token, rows):
    return pl.pallas_call(
        merge_body,
        out_shape=jax.ShapeDtypeStruct((2, rows, 5 * LANES), BF16),
        compiler_params=pltpu.CompilerParams(vmem_limit_bytes=VMEM_BYTES),
    )(x, token)


def on_device(query_in, key_in, value_in, residual, out_weight, gate_scale):
    rows = query_in.shape[0]
    core = lax.axis_index("c")
    weight = jnp.concatenate([out_weight, flip(out_weight, "c")], axis=0)
    weight = lax.optimization_barrier(weight)

    q, kv = arrange(exchange(cut(query_in, key_in, value_in, ((0, 2), (1, 3), (4, 4))), CZ))
    kv_near, q_near = neighbours(kv, "y"), neighbours(q, "x")
    parts = halves(kv_near, q_near, weight[:16, :LANES])
    kv_far, q_far = far(parts[:2], "y"), far(parts[2:], "x")

    near = jax.ShapeDtypeStruct((3, 12 * rows, LANES), F32)
    state = flash(
        near_body, [near, near], rows, 3, 9 / 32, [q, *q_near, kv, *kv_near, parts[2]]
    )
    blocks = [
        jax.ShapeDtypeStruct((16, 3, -(-(rows + 3) // 16) * 16, LANES), BF16),
        jax.ShapeDtypeStruct((8, LANES), F32),
    ]
    stage = [q, *q_near, *q_far, kv, *kv_near, *kv_far]
    scratch = [pltpu.VMEM(near.shape, F32)] * 2
    crossing, token = flash(rest_body, blocks, rows, 4, 7 / 32, [*stage, *state], scratch)
    owners = ("x", "c", "zl")
    crossing = exchange(crossing, owners)
    own, token = flash(whole_body, blocks, rows, 4, 0.5, stage + [token])
    crossing = merge(crossing, token, rows)
    def product(features):
        mine = jnp.where(core == 0, features[0], features[1])
        next_one = jnp.where(core == 0, features[1], features[0])
        wide = jnp.concatenate([mine, next_one], axis=1)
        return jnp.dot(wide, weight, preferred_element_type=F32)

    theirs = product(crossing).astype(BF16)
    own = merge(exchange(own, owners), theirs[:16, :LANES], rows)
    ours = lax.optimization_barrier(product(own))
    projected = ours + flip(theirs, "zh", "zl").astype(F32)
    return (residual.astype(F32) + gate_scale * projected).astype(BF16)


def solution(mesh):
    fine = Mesh(mesh.devices.reshape(tuple(SIZES.values())), ALL)
    tokens = P(ALL, None)
    return jax.shard_map(
        on_device,
        mesh=fine,
        in_specs=(tokens, tokens, tokens, tokens, P(("zh", "c"), None), P()),
        out_specs=tokens,
        check_vma=False,
    )
```
